32 devices in a mesh: dp: 8 (over y, x, core), head: 4 (over z).
Axes of the slice: x: 2, y: 2, z: 4, core: 2. Of those that a mesh axis runs over, the one named last changes fastest.
Arguments:
- query_rows: bfloat16 [8, 512, 3072], P('dp', 'head'), may hold values from -6 to 6
- key_rows: bfloat16 [8, 512, 3072], P('dp', 'head'), may hold values from -6 to 6
- value_rows: bfloat16 [8, 512, 3072], P('dp', 'head'), may hold values from -6 to 6
- out_grad: bfloat16 [8, 512, 6144], P('dp', 'head'), may hold values from -6 to 6
- out_weight: bfloat16 [3072, 6144], P('head', 'dp'), may hold values from -0.109375 to 0.109375
- token_order: int32 [8, 512], P('dp'), may hold values from 0 to 511, as said below
- tile_index: int32 [8, 24, 4, 4], P('dp', 'head'), may hold values from 0 to 3, as said below
- tile_count: int32 [8, 24, 4], P('dp', 'head'), may hold values from 1 to 4, as said below
Outputs:
- attention: bfloat16 [8, 512, 3072], P('dp', None, 'head')
- query_grad: bfloat16 [8, 512, 3072], P('dp', 'head')
- key_grad: bfloat16 [8, 512, 3072], P('dp', 'head')
- value_grad: bfloat16 [8, 512, 3072], P('dp', 'head')
- weight_grad: bfloat16 [3072, 6144], P('head', 'dp')
The draws below stay inside these ranges and needn't reach their ends.
Inputs may be any that keep to these rules, and one draw needn't show every extreme that they name: `token_order`: each clip's row is a permutation of the positions. `tile_index`: slot 0 of every list names the query cube itself; the entries of one list differ. Only the first tile_count[c, h, b] slots of list (c, h, b) are used.
All inputs are finite; a program needn't handle non-finite values.
Results may differ from the reference program's by a relative error of at most 0.015.
Values may be sent and summed in bfloat16 or wider, within the bound.
No kernel may reach another device: no remote copies, remote signals or barrier semaphores. Data moves between devices by JAX's collectives and lax.ppermute only.
A program may use at most 128 MiB of HBM per device.

```python
import math
import jax
import jax.numpy as jnp
from jax import lax

D = 6144
HEAD_DIM = 128
HEADS = 24
CUBE_TOKENS = 128
SLOTS = 4
SEQ = 512
CUBES = 4
HD = 3072
CLIPS = 8


def clip_orders(key):
    clip_keys = jax.random.split(jax.random.fold_in(key, 11), CLIPS)
    return jax.vmap(lambda single: jax.random.permutation(single, SEQ))(clip_keys).astype(jnp.int32)


def spread_values(key):
    values = jnp.clip(jax.random.normal(key, (CLIPS, SEQ, HD), jnp.float32), -6.0, 6.0)
    return values.astype(jnp.bfloat16)


def draw_query_rows(key, part):
    key = jax.random.fold_in(key, 1)
    return spread_values(key)


def draw_key_rows(key, part):
    key = jax.random.fold_in(key, 4)
    return spread_values(key)


def draw_token_order(key, part):
    shared = clip_orders(key)
    return shared


def draw_tile_index(key, part):
    key = jax.random.fold_in(key, 3)
    raw = jax.random.randint(key, (CLIPS, HEADS, CUBES, CUBES), 0, 1 << 20)
    cube_ids = jnp.arange(CUBES, dtype=jnp.int32)
    ranked = raw * CUBES + cube_ids
    ranked = jnp.where(cube_ids[:, None] == cube_ids[None, :], -1, ranked)
    return jnp.argsort(ranked, axis=-1, stable=True)[..., :SLOTS].astype(jnp.int32)


def draw_tile_count(key, part):
    key = jax.random.fold_in(key, 5)
    cap_key, count_key, head_key, cube_key = jax.random.split(key, 4)
    head_caps = jax.random.randint(cap_key, (CLIPS, HEADS, 1), 1, SLOTS + 1)
    counts = 1 + jax.random.randint(count_key, (CLIPS, HEADS, CUBES), 0, head_caps)
    full_head = jax.random.randint(head_key, (CLIPS, 1, 1), 0, HEADS)
    full_cube = jax.random.randint(cube_key, (CLIPS, 1, 1), 0, CUBES)
    chosen = (jnp.arange(HEADS)[None, :, None] == full_head) & (jnp.arange(CUBES)[None, None, :] == full_cube)
    return jnp.where(chosen, SLOTS, counts).astype(jnp.int32)


def with_spikes(drawn, rng, source, target, shards_of, factor):
    def block_of(position):
        return (jnp.arange(drawn.shape[position]) // (drawn.shape[position] // shards_of)).reshape((-1,) + (1,) * (drawn.ndim - 1 - position))

    near = jax.random.permutation(rng, shards_of)[block_of(target)]
    second = (block_of(target) + shards_of // 2) % shards_of
    return jnp.where((block_of(source) == near) | (block_of(source) == second), factor * drawn, drawn)


def shard_levels(key, extent, pieces, low, top_value):
    loudness, own = 1.0, jax.random.fold_in(key, 6)
    for position, shards_of in pieces:
        draws = jnp.exp(jax.random.uniform(jax.random.fold_in(own, position), (shards_of,), jnp.float32, low / len(pieces), top_value / len(pieces)))
        loudness = loudness * jnp.repeat(draws, extent[position] // shards_of).reshape([-1 if axis == position else 1 for axis in range(len(extent))])
    return loudness


def normal_values(rng, extent, scale, limit, cuts=(), kind=jnp.bfloat16):
    values = jax.random.normal(rng, extent, jnp.float32) * scale
    if len(cuts) > 0:
        values = shard_levels(rng, extent, cuts, -0.22, 0.18) * values
    return jnp.clip(values, min=-limit, max=limit).astype(kind)


def bell_draw_with(stream_key, shape, deviation, bound, shards, heavy, kind=jnp.bfloat16):
    values = deviation * jax.random.normal(stream_key, shape, jnp.float32)
    if shards:
        values = values * shard_levels(stream_key, shape, shards, -0.22, 0.18)
    return jnp.clip(with_spikes(values, jax.random.fold_in(stream_key, 3), *heavy), -bound, bound).astype(kind)


def setup_inputs(seed: int = 0) -> dict:
    streams_of = jax.random.split(jax.random.key(seed), 9)
    query_rows = draw_query_rows(jax.random.fold_in(streams_of[8], 71), 0)
    key_rows = draw_key_rows(jax.random.fold_in(streams_of[8], 71), 0)
    value_rows = normal_values(streams_of[2], (CLIPS, SEQ, HD), 1.0, 6.0, ((0, 8), (1, 4)))
    out_grad = bell_draw_with(streams_of[3], (CLIPS, SEQ, D), 1.0, 6.0, ((0, 8), (1, 4)), (0, 2, 8, 2.0))
    out_weight = normal_values(streams_of[4], (HD, D), HD ** -0.5, 0.109375, ((0, 4), (1, 8)))
    token_order = draw_token_order(jax.random.fold_in(streams_of[8], 71), 0)
    tile_index = draw_tile_index(jax.random.fold_in(streams_of[8], 71), 0)
    tile_count = draw_tile_count(jax.random.fold_in(streams_of[8], 71), 0)
    return dict(query_rows=query_rows, key_rows=key_rows, value_rows=value_rows, out_grad=out_grad, out_weight=out_weight, token_order=token_order, tile_index=tile_index, tile_count=tile_count)


masked_score = -1e+30

def tile_pass(query_cubes, key_cubes, value_cubes, grad_cubes, tiles, counts):
    heads_here, cube_count, slot_total = tiles.shape
    scale = 1.0 / math.sqrt(query_cubes.shape[-1])
    head_ids = jnp.arange(heads_here, dtype=jnp.int32)[:, None, None]
    key_tiles = key_cubes[head_ids, tiles].astype(jnp.float32)
    value_tiles = value_cubes[head_ids, tiles].astype(jnp.float32)
    query_float = query_cubes.astype(jnp.float32)
    grad_float = grad_cubes.astype(jnp.float32)
    living = (jnp.arange(slot_total, dtype=jnp.int32)[None, None, :] < counts[:, :, None])[:, :, None, :, None]
    scores = jnp.einsum('hcqd,hcjkd->hcqjk', query_float, key_tiles) * scale
    scores = jnp.where(living, scores, masked_score)
    maxima = lax.optimization_barrier(jnp.max(scores, axis=(3, 4), keepdims=True))
    log_total = maxima + jnp.log(lax.optimization_barrier(jnp.sum(jnp.exp(scores - maxima), axis=(3, 4), keepdims=True)))
    weights = jnp.exp(scores - log_total)
    weights_bf = weights.astype(jnp.bfloat16).astype(jnp.float32)
    output = jnp.einsum('hcqjk,hcjkd->hcqd', weights_bf, value_tiles).astype(jnp.bfloat16)
    delta = lax.optimization_barrier(jnp.sum(grad_float * output.astype(jnp.float32), axis=-1))[..., None, None]
    grad_scores = jnp.einsum('hcqd,hcjkd->hcqjk', grad_float, value_tiles)
    diff_bf = (weights * (grad_scores - delta)).astype(jnp.bfloat16).astype(jnp.float32)
    query_grad = (jnp.einsum('hcqjk,hcjkd->hcqd', diff_bf, key_tiles) * scale).astype(jnp.bfloat16)
    onehot = (tiles[..., None] == jnp.arange(cube_count, dtype=jnp.int32)).astype(jnp.float32)
    key_parts = jnp.einsum('hcqjk,hcqd->hcjkd', diff_bf, query_float) * scale
    value_parts = jnp.einsum('hcqjk,hcqd->hcjkd', weights_bf, grad_float)
    key_grad = jnp.einsum('hcjb,hcjkd->hbkd', onehot, key_parts, precision=lax.Precision.HIGHEST).astype(jnp.bfloat16)
    value_grad = jnp.einsum('hcjb,hcjkd->hbkd', onehot, value_parts, precision=lax.Precision.HIGHEST).astype(jnp.bfloat16)
    return (output, query_grad, key_grad, value_grad)

def reference(query_rows, key_rows, value_rows, out_grad, out_weight, token_order, tile_index, tile_count):

    def one_clip(inputs):
        queries, keys_here, values, grads, order, tiles, counts = inputs

        def to_cubes(rows):
            return rows[order].reshape(CUBES, CUBE_TOKENS, HEADS, HEAD_DIM).transpose(2, 0, 1, 3)

        def to_rows(cubes):
            flat = cubes.transpose(1, 2, 0, 3).reshape(SEQ, HD)
            return jnp.zeros_like(flat).at[order].set(flat)
        grad_heads = lax.dot_general(grads, out_weight, (((1,), (1,)), ((), ())), preferred_element_type=jnp.float32).astype(jnp.bfloat16)
        output, query_grad, key_grad, value_grad = tile_pass(to_cubes(queries), to_cubes(keys_here), to_cubes(values), to_cubes(grad_heads), tiles, counts)
        return (to_rows(output), to_rows(query_grad), to_rows(key_grad), to_rows(value_grad))
    attention, query_grad, key_grad, value_grad = lax.map(one_clip, (query_rows, key_rows, value_rows, out_grad, token_order, tile_index, tile_count))
    weight_grad = lax.dot_general(attention.reshape(CLIPS * SEQ, HD), out_grad.reshape(CLIPS * SEQ, D), (((0,), (0,)), ((), ())), preferred_element_type=jnp.float32).astype(jnp.bfloat16)
    return (attention, query_grad, key_grad, value_grad, weight_grad)
```

```python
import functools
import math

import jax
import jax.numpy as jnp
from jax import lax
from jax.experimental import pallas as pl
from jax.experimental.pallas import tpu as pltpu
from jax.sharding import PartitionSpec as P

HEAD_DIM = 128
CUBE_TOKENS = 128
LANES = 128
CHUNKS = 3

masked_score = -1e30
scale = 1.0 / math.sqrt(HEAD_DIM)
log2_e = math.log2(math.e)

BF16 = jnp.bfloat16
F32 = jnp.float32
NT = (((1,), (1,)), ((), ()))
NN = (((1,), (0,)), ((), ()))


def dot(a, b, dims=NN):
    return lax.dot_general(a, b, dims, preferred_element_type=F32)


def params(limit_mib=48):
    return pltpu.CompilerParams(vmem_limit_bytes=limit_mib * 1024 * 1024)


def bit_reversed(count):
    bits = count.bit_length() - 1
    return [sum(((p >> i) & 1) << (bits - 1 - i) for i in range(bits)) for p in range(count)]


def pack_kernel(place, q_ref, k_ref, v_ref, *outs):
    width = outs[0].shape[2]
    for s, out in enumerate(outs):
        columns = pl.ds(pl.multiple_of(place[s] * width, LANES), width)
        for i, rows in enumerate((q_ref, k_ref, v_ref)):
            out[i] = rows[0, :, columns]


def pack(place, q, k, v):
    group = place.shape[0]
    rows, total = q.shape[1:]
    shape = jax.ShapeDtypeStruct((3, rows, total // group), BF16)
    return pl.pallas_call(
        pack_kernel,
        out_shape=[shape] * group,
        grid_spec=pltpu.PrefetchScalarGridSpec(
            num_scalar_prefetch=1,
            in_specs=[pl.BlockSpec(memory_space=pltpu.VMEM)] * 3,
            out_specs=[pl.BlockSpec(memory_space=pltpu.VMEM)] * group,
        ),
        compiler_params=params(),
    )(place, q, k, v)


def unpack_kernel(group, place, *refs):
    parts, outs = refs[:group], refs[group:]
    width = parts[0].shape[2]
    for s, part in enumerate(parts):
        columns = pl.ds(pl.multiple_of(place[s] * width, LANES), width)
        for i, out in enumerate(outs):
            out[0, :, columns] = part[i]


def unpack(place, parts):
    group = place.shape[0]
    _, rows, width = parts[0].shape
    shape = jax.ShapeDtypeStruct((1, rows, width * group), BF16)
    return pl.pallas_call(
        functools.partial(unpack_kernel, group),
        out_shape=[shape] * 3,
        grid_spec=pltpu.PrefetchScalarGridSpec(
            num_scalar_prefetch=1,
            in_specs=[pl.BlockSpec(memory_space=pltpu.VMEM)] * group,
            out_specs=[pl.BlockSpec(memory_space=pltpu.VMEM)] * 3,
        ),
        compiler_params=params(),
    )(place, *parts)


def forward_kernel(group, place, order_ref, bias_ref, *refs):
    parts = refs[:group]
    att_ref, att_t_ref, weight_ref, q_t_ref, k_ref, v_ref, cube_ref, q_ref = refs[group:]
    rows = parts[0].shape[1]
    total = q_ref.shape[0]

    @pl.when(pl.program_id(0) == 0)
    def _():
        token = lax.broadcasted_iota(jnp.int32, (total, total), 0)
        onehot = jnp.where(token == order_ref[...], 1.0, 0.0).astype(BF16)
        position = lax.broadcasted_iota(jnp.int32, (total, LANES), 0)
        cube = lax.broadcasted_iota(jnp.int32, (total, LANES), 1)
        block = jnp.where(lax.div(position, CUBE_TOKENS) == cube, 1.0, 0.0).astype(BF16)
        cube_ref[...] = dot(onehot, block).astype(BF16)

    for s, part in enumerate(parts):
        here = pl.ds(pl.multiple_of(place[s] * rows, rows), rows)
        q_ref[here, :] = part[0]
        k_ref[here, :] = part[1]
        v_ref[here, :] = part[2]
    cubes = cube_ref[...]
    q, k, v = q_ref[...], k_ref[...], v_ref[...]
    bias = dot(cubes, bias_ref[0]).astype(BF16)
    scores = dot(
        jnp.concatenate([q, bias], axis=1), jnp.concatenate([k, cubes], axis=1), NT
    ) * (scale * log2_e)
    raised = jnp.exp2(scores - jnp.max(scores, axis=1, keepdims=True))
    weights = (raised * (1.0 / jnp.sum(raised, axis=1, keepdims=True))).astype(BF16)
    weight_ref[0] = weights
    output = dot(weights, v)
    att_ref[...] = output.astype(BF16)
    att_t_ref[...] = output.T.astype(BF16)
    q_t_ref[...] = q.astype(F32).T.astype(BF16)


def forward(place, order, bias, parts):
    group = place.shape[0]
    _, rows, width = parts[0].shape
    total = rows * group
    heads = width // HEAD_DIM
    column = pl.BlockSpec((total, HEAD_DIM), lambda h, *_: (0, h))
    row = pl.BlockSpec((HEAD_DIM, total), lambda h, *_: (h, 0))
    return pl.pallas_call(
        functools.partial(forward_kernel, group),
        out_shape=[
            jax.ShapeDtypeStruct((total, width), BF16),
            jax.ShapeDtypeStruct((width, total), BF16),
            jax.ShapeDtypeStruct((heads, total, total), BF16),
            jax.ShapeDtypeStruct((width, total), BF16),
            jax.ShapeDtypeStruct((total, width), BF16),
            jax.ShapeDtypeStruct((total, width), BF16),
        ],
        grid_spec=pltpu.PrefetchScalarGridSpec(
            num_scalar_prefetch=1,
            grid=(heads,),
            in_specs=[
                pl.BlockSpec((1, total), lambda h, *_: (0, 0)),
                pl.BlockSpec((1, LANES, LANES), lambda h, *_: (h, 0, 0)),
            ]
            + [pl.BlockSpec((3, rows, HEAD_DIM), lambda h, *_: (0, 0, h))] * group,
            out_specs=[
                column,
                row,
                pl.BlockSpec((1, total, total), lambda h, *_: (h, 0, 0)),
                row,
                column,
                column,
            ],
            scratch_shapes=[
                pltpu.VMEM((total, LANES), BF16),
                pltpu.VMEM((total, HEAD_DIM), BF16),
            ],
        ),
        compiler_params=params(),
    )(place, order, bias, *parts)


def backward_kernel(group, place, g_ref, att_ref, weight_ref, q_t_ref, k_ref, v_ref, *refs):
    outs, held = refs[:group], refs[group]
    rows = outs[0].shape[1]
    grad = g_ref[...]
    weights = weight_ref[0]
    grad_float = grad.astype(F32)
    delta = jnp.sum(grad_float * att_ref[...].astype(F32), axis=1, keepdims=True)
    diff = (weights.astype(F32) * (dot(grad, v_ref[...], NT) - delta)).astype(BF16)
    held[0] = (dot(diff, k_ref[...]) * scale).astype(BF16)
    held[1] = (dot(q_t_ref[...], diff) * scale).T.astype(BF16)
    held[2] = dot(grad_float.T.astype(BF16), weights).T.astype(BF16)
    for s, out in enumerate(outs):
        here = pl.ds(pl.multiple_of(place[s] * rows, rows), rows)
        out[...] = held[:, here, :]


def backward(place, grad, att, weights, q_t, k, v):
    group = place.shape[0]
    total, width = grad.shape
    rows = total // group
    heads = width // HEAD_DIM
    column = pl.BlockSpec((total, HEAD_DIM), lambda h, *_: (0, h))
    row = pl.BlockSpec((HEAD_DIM, total), lambda h, *_: (h, 0))
    return pl.pallas_call(
        functools.partial(backward_kernel, group),
        out_shape=[jax.ShapeDtypeStruct((3, rows, width), BF16)] * group,
        grid_spec=pltpu.PrefetchScalarGridSpec(
            num_scalar_prefetch=1,
            grid=(heads,),
            in_specs=[
                column,
                column,
                pl.BlockSpec((1, total, total), lambda h, *_: (h, 0, 0)),
                row,
                column,
                column,
            ],
            out_specs=[pl.BlockSpec((3, rows, HEAD_DIM), lambda h, *_: (0, 0, h))] * group,
            scratch_shapes=[pltpu.VMEM((3, total, HEAD_DIM), BF16)],
        ),
        compiler_params=params(),
    )(place, grad, att, weights, q_t, k, v)


def project_kernel(count, blocks, rows_ref, *refs):
    weights, before, out = refs[:count], refs[count:-1], refs[-1]
    width = weights[0].shape[1]
    total = before[0][...] if before else None
    for p, weight in enumerate(weights):
        columns = pl.ds(pl.multiple_of(blocks[p] * width, LANES), width)
        term = dot(rows_ref[:, columns], weight[...], NT)
        total = term if total is None else total + term
    out[...] = total.astype(out.dtype)


def project(blocks, rows, weights, chunk, before, dtype):
    count = len(weights)
    tokens, width = rows.shape[0], rows.shape[1] // count
    heads = weights[0].shape[0]
    before = [] if before is None else [before]
    whole = pl.BlockSpec((tokens, heads), lambda i, *_: (0, 0))
    return pl.pallas_call(
        functools.partial(project_kernel, count),
        out_shape=jax.ShapeDtypeStruct((tokens, heads), dtype),
        grid_spec=pltpu.PrefetchScalarGridSpec(
            num_scalar_prefetch=1,
            grid=(1,),
            in_specs=[pl.BlockSpec(rows.shape, lambda i, *_: (0, 0))]
            + [pl.BlockSpec((heads, width), lambda i, *_: (0, chunk))] * count
            + [whole] * len(before),
            out_specs=whole,
        ),
        compiler_params=params(),
    )(blocks, rows, *weights, *before)


def outer_kernel(blocks, att_t_ref, rows_ref, keep_ref, send_ref):
    half, _, width = keep_ref.shape
    att_t = att_t_ref[...]
    for p in range(2 * half):
        columns = pl.ds(pl.multiple_of(blocks[p] * width, LANES), width)
        out = keep_ref if p < half else send_ref
        out[p % half] = dot(att_t, rows_ref[:, columns]).astype(BF16)


def outer(blocks, att_t, rows):
    count = blocks.shape[0]
    heads, width = att_t.shape[0], rows.shape[1] // count
    shape = jax.ShapeDtypeStruct((count // 2, heads, width), BF16)
    return pl.pallas_call(
        outer_kernel,
        out_shape=[shape] * 2,
        grid_spec=pltpu.PrefetchScalarGridSpec(
            num_scalar_prefetch=1,
            in_specs=[pl.BlockSpec(memory_space=pltpu.VMEM)] * 2,
            out_specs=[pl.BlockSpec(memory_space=pltpu.VMEM)] * 2,
        ),
        compiler_params=params(),
    )(blocks, att_t, rows)


def swap(value, axis, size, mask):
    return lax.ppermute(value, axis, [(i, i ^ mask) for i in range(size)])


def scatter_sum(keep, send, dp):
    steps = dp.bit_length() - 1
    kept = keep.astype(F32)
    for step in range(steps):
        arrived = swap(send, "dp", dp, 1 << step).astype(F32)
        kept = kept + arrived
        if step < steps - 1:
            half = kept.shape[0] // 2
            send, kept = kept[half:].astype(BF16), kept[:half]
    return kept[0].astype(BF16)


def gather_weight(weight, dp):
    held = [weight]
    mask = dp // 2
    while mask:
        held = held + [swap(part, "dp", dp, mask) for part in held]
        mask //= 2
    return held


def local(
    dp,
    group,
    query_rows,
    key_rows,
    value_rows,
    out_grad,
    out_weight,
    token_order,
    tile_index,
    tile_count,
):
    tokens_here, model = out_grad.shape[1:]
    part = model // dp // CHUNKS
    place = jnp.bitwise_xor(lax.axis_index("head"), jnp.arange(group, dtype=jnp.int32))
    blocks = jnp.bitwise_xor(lax.axis_index("dp"), jnp.array(bit_reversed(dp), jnp.int32))

    packed = pack(place, query_rows, key_rows, value_rows)
    parts = [packed[0]] + [swap(packed[s], "head", group, s) for s in range(1, group)]

    pieces = out_grad.reshape(tokens_here, dp, CHUNKS, part)
    gathered = [
        lax.all_gather(
            pieces[:, :, j].reshape(tokens_here, dp * part), "head", axis=0, tiled=True
        )
        for j in range(CHUNKS)
    ]
    weights_full = gather_weight(out_weight, dp)

    tiles, counts = tile_index[0], tile_count[0]
    heads, cubes, slots = tiles.shape
    used = jnp.arange(slots, dtype=jnp.int32) < counts[:, :, None]
    listed = tiles[..., None] == jnp.arange(LANES, dtype=jnp.int32)
    allowed = jnp.any(listed & used[..., None], axis=2)
    bias = jnp.where(allowed, 0.0, masked_score).astype(BF16)
    bias = jnp.pad(bias, ((0, 0), (0, LANES - cubes), (0, 0)))

    att, att_t, weights, q_t, k, v = forward(place, token_order, bias, parts)

    grad = None
    sums = []
    for j in range(CHUNKS):
        last = j == CHUNKS - 1
        grad = project(blocks, gathered[j], weights_full, j, grad, BF16 if last else F32)
        sums.append(scatter_sum(*outer(blocks, att_t, gathered[j]), dp))

    back = backward(place, grad, att, weights, q_t, k, v)
    back = [back[0]] + [swap(back[s], "head", group, s) for s in range(1, group)]
    query_back, key_back, value_back = unpack(place, back)
    return (att[None], query_back, key_back, value_back, jnp.concatenate(sums, axis=1))


def solution(mesh):
    placed = (
        P("dp", "head", None),
        P("dp", "head", None),
        P("dp", "head", None),
        P("dp", "head", None),
        P("head", "dp"),
        P("dp", None),
        P("dp", "head", None, None),
        P("dp", "head", None),
    )
    return jax.shard_map(
        functools.partial(local, mesh.shape["dp"], mesh.shape["head"]),
        mesh=mesh,
        in_specs=placed,
        out_specs=(
            P("dp", None, "head"),
            P("dp", "head", None),
            P("dp", "head", None),
            P("dp", "head", None),
            P("head", "dp"),
        ),
        check_vma=False,
    )
```

```python
import functools
import math

import jax
import jax.numpy as jnp
from jax import lax
from jax.experimental import pallas as pl
from jax.experimental.pallas import tpu as pltpu
from jax.sharding import PartitionSpec as P

HEAD_DIM = 128
CUBE_TOKENS = 128
LANES = 128

masked_score = -1e30
scale = 1.0 / math.sqrt(HEAD_DIM)
log2_e = math.log2(math.e)

BF16 = jnp.bfloat16
F32 = jnp.float32
NT = (((1,), (1,)), ((), ()))
NN = (((1,), (0,)), ((), ()))


def chunk_widths(columns):
    return [columns // 3] * 3


def light():
    return pl.CostEstimate(flops=1, bytes_accessed=1, transcendentals=0)


def whole(shape):
    return pl.BlockSpec(shape, lambda *_: (0,) * len(shape))


def awaited(after):
    return [pl.BlockSpec(memory_space=pl.ANY)] * len(after)


def dot(a, b, dims=NN):
    return lax.dot_general(a, b, dims, preferred_element_type=F32)


def params(limit_mib=60):
    return pltpu.CompilerParams(vmem_limit_bytes=limit_mib * 1024 * 1024)


def tables(group, here):
    partner = jnp.bitwise_xor(here, jnp.arange(group, dtype=jnp.int32))
    if group != 4:
        return jnp.concatenate([partner, partner, jnp.arange(group, dtype=jnp.int32)])
    middle = jnp.logical_or(here == 1, here == 2)
    slots = jnp.where(middle, jnp.array([0, 1, 3, 2], jnp.int32), jnp.arange(4, dtype=jnp.int32))
    return jnp.concatenate([partner, slots, jnp.bitwise_xor(here, slots)])


def slot(table, s):
    return table[table.shape[0] // 3 + s]


def owner(table, t):
    return table[table.shape[0] // 3 * 2 + t]


def pack_kernel(group, table, *refs):
    ins, outs = refs[: 3 * group], refs[-group:]
    for s, out in enumerate(outs):
        for i in range(3):
            out[i] = ins[3 * s + i][0]


def pack(table, q, k, v, after=()):
    group = table.shape[0] // 3
    rows, total = q.shape[1:]
    shape = (3, rows, total // group)
    in_specs = []
    for s in range(group):
        in_specs += [
            pl.BlockSpec((1, rows, total // group), lambda i, t, s=s: (0, 0, t[s]))
        ] * 3
    return pl.pallas_call(
        functools.partial(pack_kernel, group),
        out_shape=[jax.ShapeDtypeStruct(shape, BF16)] * group,
        grid_spec=pltpu.PrefetchScalarGridSpec(
            num_scalar_prefetch=1,
            grid=(1,),
            in_specs=in_specs + awaited(after),
            out_specs=[whole(shape)] * group,
        ),
        cost_estimate=light(),
        compiler_params=params(),
    )(table, *[q, k, v] * group, *after)


def split_kernel(dp, g_ref, *outs):
    columns = g_ref.shape[2] // dp
    before = 0
    for out in outs:
        part = out.shape[1] // dp
        for d in range(dp):
            start = d * columns + before
            out[:, d * part : (d + 1) * part] = g_ref[0, :, start : start + part]
        before += part


def split(g, dp):
    shapes = [(g.shape[1], width * dp) for width in chunk_widths(g.shape[2] // dp)]
    return pl.pallas_call(
        functools.partial(split_kernel, dp),
        out_shape=[jax.ShapeDtypeStruct(shape, BF16) for shape in shapes],
        grid=(1,),
        in_specs=[whole(g.shape)],
        out_specs=[whole(shape) for shape in shapes],
        cost_estimate=light(),
        compiler_params=params(),
    )(g)


def join_kernel(a_ref, b_ref, *refs):
    out = refs[-1]
    out[: a_ref.shape[0]] = a_ref[...]
    out[a_ref.shape[0] :] = b_ref[...]


def join(a, b, after=()):
    shape = (a.shape[0] + b.shape[0],) + a.shape[1:]
    return pl.pallas_call(
        join_kernel,
        out_shape=jax.ShapeDtypeStruct(shape, a.dtype),
        grid=(1,),
        in_specs=[whole(a.shape), whole(b.shape)] + awaited(after),
        out_specs=whole(shape),
        cost_estimate=light(),
        compiler_params=params(),
    )(a, b, *after)


def hold_kernel(*refs):
    pass


def hold(value, after):
    return pl.pallas_call(
        hold_kernel,
        out_shape=jax.ShapeDtypeStruct(value.shape, value.dtype),
        in_specs=awaited([value, *after]),
        out_specs=pl.BlockSpec(memory_space=pl.ANY),
        input_output_aliases={0: 0},
        cost_estimate=light(),
        compiler_params=params(),
    )(value, *after)


def unpack_kernel(group, place, *refs):
    parts, outs = refs[:group], refs[-3:]
    width = parts[0].shape[2]
    for s, part in enumerate(parts):
        columns = pl.ds(pl.multiple_of(place[s] * width, LANES), width)
        for i, out in enumerate(outs):
            out[0, :, columns] = part[i]


def unpack(place, parts, after=()):
    group = place.shape[0] // 3
    _, rows, width = parts[0].shape
    shape = jax.ShapeDtypeStruct((1, rows, width * group), BF16)
    return pl.pallas_call(
        functools.partial(unpack_kernel, group),
        out_shape=[shape] * 3,
        grid_spec=pltpu.PrefetchScalarGridSpec(
            num_scalar_prefetch=1,
            grid=(1,),
            in_specs=[whole(part.shape) for part in parts] + awaited(after),
            out_specs=[whole(shape.shape)] * 3,
        ),
        cost_estimate=light(),
        compiler_params=params(),
    )(place, *parts, *after)


def forward_kernel(group, table, order_ref, bias_ref, *refs):
    parts = refs[:group]
    att_ref, att_t_ref, weight_ref, q_t_ref, k_ref, v_ref, cube_ref, q_ref = refs[-8:]
    rows = parts[0].shape[1]
    total = q_ref.shape[0]

    @pl.when(pl.program_id(0) == 0)
    def _():
        position = lax.broadcasted_iota(jnp.int32, (total, LANES), 0)
        cube = lax.broadcasted_iota(jnp.int32, (total, LANES), 1)
        block = jnp.where(lax.div(position, CUBE_TOKENS) == cube, 1.0, 0.0).astype(BF16)
        for t in range(group):
            token = lax.broadcasted_iota(jnp.int32, (rows, total), 0) + owner(table, t) * rows
            onehot = jnp.where(token == order_ref[...], 1.0, 0.0).astype(BF16)
            cube_ref[t * rows : (t + 1) * rows, :] = dot(onehot, block).astype(BF16)

    for s, part in enumerate(parts):
        here = pl.ds(pl.multiple_of(slot(table, s) * rows, rows), rows)
        q_ref[here, :] = part[0]
        k_ref[here, :] = part[1]
        v_ref[here, :] = part[2]
    cubes = cube_ref[...]
    q, k, v = q_ref[...], k_ref[...], v_ref[...]
    bias = dot(cubes, bias_ref[0]).astype(BF16)
    scores = dot(
        jnp.concatenate([q, bias], axis=1), jnp.concatenate([k, cubes], axis=1), NT
    ) * (scale * log2_e)
    raised = jnp.exp2(scores - jnp.max(scores, axis=1, keepdims=True))
    weights = (raised * (1.0 / jnp.sum(raised, axis=1, keepdims=True))).astype(BF16)
    weight_ref[0] = weights
    output = dot(weights, v)
    for t in range(group):
        here = pl.ds(pl.multiple_of(owner(table, t) * rows, rows), rows)
        att_ref[here, :] = output[t * rows : (t + 1) * rows].astype(BF16)
    att_t_ref[...] = output.T.astype(BF16)
    q_t_ref[...] = q.astype(F32).T.astype(BF16)


def forward(table, order, bias, parts, after=()):
    group = len(parts)
    _, rows, width = parts[0].shape
    total = rows * group
    heads = width // HEAD_DIM
    column = pl.BlockSpec((total, HEAD_DIM), lambda h, *_: (0, h))
    row = pl.BlockSpec((HEAD_DIM, total), lambda h, *_: (h, 0))
    return pl.pallas_call(
        functools.partial(forward_kernel, group),
        out_shape=[
            jax.ShapeDtypeStruct((total, width), BF16),
            jax.ShapeDtypeStruct((width, total), BF16),
            jax.ShapeDtypeStruct((heads, total, total), BF16),
            jax.ShapeDtypeStruct((width, total), BF16),
            jax.ShapeDtypeStruct((total, width), BF16),
            jax.ShapeDtypeStruct((total, width), BF16),
        ],
        grid_spec=pltpu.PrefetchScalarGridSpec(
            num_scalar_prefetch=1,
            grid=(heads,),
            in_specs=[
                pl.BlockSpec((1, total), lambda h, *_: (0, 0)),
                pl.BlockSpec((1, LANES, LANES), lambda h, *_: (h, 0, 0)),
            ]
            + [pl.BlockSpec((3, rows, HEAD_DIM), lambda h, *_: (0, 0, h))] * group
            + awaited(after),
            out_specs=[
                column,
                row,
                pl.BlockSpec((1, total, total), lambda h, *_: (h, 0, 0)),
                row,
                column,
                column,
            ],
            scratch_shapes=[
                pltpu.VMEM((total, LANES), BF16),
                pltpu.VMEM((total, HEAD_DIM), BF16),
            ],
        ),
        cost_estimate=light(),
        compiler_params=params(),
    )(table, order, bias, *parts, *after)


def backward_kernel(
    group, passed, table, g_ref, att_ref, weight_ref, q_t_ref, k_ref, v_ref, *refs
):
    outs, held = refs[passed : passed + group], refs[-1]
    rows = outs[0].shape[1]
    grad = g_ref[...]
    weights = weight_ref[0]
    grad_float = grad.astype(F32)
    att = jnp.concatenate(
        [
            att_ref[pl.ds(pl.multiple_of(owner(table, t) * rows, rows), rows), :]
            for t in range(group)
        ],
        axis=0,
    )
    delta = jnp.sum(grad_float * att.astype(F32), axis=1, keepdims=True)
    diff = (weights.astype(F32) * (dot(grad, v_ref[...], NT) - delta)).astype(BF16)
    held[0] = (dot(diff, k_ref[...]) * scale).astype(BF16)
    held[1] = (dot(q_t_ref[...], diff) * scale).T.astype(BF16)
    held[2] = dot(grad_float.T.astype(BF16), weights).T.astype(BF16)
    for s, out in enumerate(outs):
        here = pl.ds(pl.multiple_of(slot(table, s) * rows, rows), rows)
        out[...] = held[:, here, :]


def backward(table, grad, att, weights, q_t, k, v, passed):
    group = table.shape[0] // 3
    total, width = grad.shape
    rows = total // group
    heads = width // HEAD_DIM
    column = pl.BlockSpec((total, HEAD_DIM), lambda h, *_: (0, h))
    row = pl.BlockSpec((HEAD_DIM, total), lambda h, *_: (h, 0))
    return pl.pallas_call(
        functools.partial(backward_kernel, group, len(passed)),
        out_shape=[jax.ShapeDtypeStruct((3, rows, width), BF16)] * group
        + [jax.ShapeDtypeStruct(x.shape, x.dtype) for x in passed],
        grid_spec=pltpu.PrefetchScalarGridSpec(
            num_scalar_prefetch=1,
            grid=(heads,),
            in_specs=[
                column,
                column,
                pl.BlockSpec((1, total, total), lambda h, *_: (h, 0, 0)),
                row,
                column,
                column,
            ]
            + awaited(passed),
            out_specs=[pl.BlockSpec((3, rows, HEAD_DIM), lambda h, *_: (0, 0, h))] * group
            + awaited(passed),
            scratch_shapes=[pltpu.VMEM((3, total, HEAD_DIM), BF16)],
        ),
        input_output_aliases={7 + i: group + i for i in range(len(passed))},
        cost_estimate=light(),
        compiler_params=params(),
    )(table, grad, att, weights, q_t, k, v, *passed)


def block_rows(refs, columns):
    if len(refs) == 1:
        return refs[0][:, columns]
    own, near, inner, outer = refs
    return jnp.concatenate(
        [own[:, columns], near[:, columns], inner[:, columns] + outer[:, columns]], axis=0
    )


def block_columns(blocks, p, width):
    return pl.ds(pl.multiple_of(blocks[p] * width, LANES), width)


def project_kernel(count, pieces, first, *refs):
    weights, refs = refs[:pieces], refs[pieces:]
    rows, out = refs[:count], refs[-1]
    dp, _, unit = weights[0].shape
    part = unit * pieces
    total = None if first else refs[count][...]
    for p in range(dp):
        weight = jnp.concatenate([w[p] for w in weights], axis=1)
        term = dot(block_rows(rows, slice(p * part, (p + 1) * part)), weight, NT)
        total = term if total is None else total + term
    out[...] = total.astype(out.dtype)


def project(rows, weights, start, before, dtype, after=()):
    dp, heads, _ = weights.shape
    part = rows[0].shape[1] // dp
    unit = math.gcd(start, part)
    tokens = sum(r.shape[0] for r in rows[:3])
    before = [] if before is None else [before]
    at = range(start // unit, (start + part) // unit)
    return pl.pallas_call(
        functools.partial(project_kernel, len(rows), len(at), not before),
        out_shape=jax.ShapeDtypeStruct((tokens, heads), dtype),
        grid=(1,),
        in_specs=[pl.BlockSpec((dp, heads, unit), lambda i, c=c: (0, 0, c)) for c in at]
        + [whole(r.shape) for r in rows]
        + [whole(x.shape) for x in before]
        + awaited(after),
        out_specs=whole((tokens, heads)),
        cost_estimate=light(),
        compiler_params=params(),
    )(*[weights] * len(at), *rows, *before, *after)


def outer_kernel(count, blocks, att_t_ref, *refs):
    rows, (keep_ref, send_ref) = refs[:count], refs[-2:]
    half, _, part = keep_ref.shape
    att_t = att_t_ref[...]
    for p in range(2 * half):
        out = keep_ref if p < half else send_ref
        here = block_rows(rows, block_columns(blocks, p, part))
        out[p % half] = dot(att_t, here).astype(BF16)


def outer(blocks, att_t, rows, start, width, buffers=()):
    half = blocks.shape[0] // 2
    heads = att_t.shape[0]
    part = rows[0].shape[1] // (2 * half)
    first = 2 + len(rows)
    return pl.pallas_call(
        functools.partial(outer_kernel, len(rows)),
        out_shape=[jax.ShapeDtypeStruct((half, heads, width), BF16)] * 2,
        grid_spec=pltpu.PrefetchScalarGridSpec(
            num_scalar_prefetch=1,
            grid=(1,),
            in_specs=[whole(att_t.shape)] + [whole(r.shape) for r in rows] + awaited(buffers),
            out_specs=[pl.BlockSpec((half, heads, part), lambda i, b: (0, 0, start // part))] * 2,
        ),
        input_output_aliases={first + i: i for i in range(len(buffers))},
        cost_estimate=light(),
        compiler_params=params(),
    )(blocks, att_t, *rows, *buffers)


def swap(value, axis, size, mask):
    return lax.ppermute(value, axis, [(i, i ^ mask) for i in range(size)])


def half_order(masks):
    order = [0]
    for mask in reversed(masks):
        order = order + [mask ^ r for r in order]
    return order


def fold(state, dp):
    kept, send, masks = state
    if not masks:
        return state
    kept = kept.astype(F32) + swap(send, "dp", dp, masks[0]).astype(F32)
    half = kept.shape[0] // 2
    if half == 0:
        kept = kept[0].astype(BF16)
        return kept, kept, masks[1:]
    return kept[:half], kept[half:].astype(BF16), masks[1:]


def gather_rows(own, near, group, both=None, held=()):
    if group != 4:
        return [lax.all_gather(own, "head", axis=0, tiled=True)]
    inner = lax.ppermute(join(own, near) if both is None else both, "head", [(1, 2), (2, 1)])
    if held:
        inner = hold(inner, held)
    outer = lax.ppermute(inner, "head", [(1, 0), (2, 3)])
    return [own, near, inner, outer]


def local(
    dp,
    group,
    query_rows,
    key_rows,
    value_rows,
    out_grad,
    out_weight,
    token_order,
    tile_index,
    tile_count,
):
    table = tables(group, lax.axis_index("head"))
    up = [1 << i for i in range(dp.bit_length() - 1)]
    masks = [up, up[:1] + up[:0:-1]]
    widths = chunk_widths(out_weight.shape[1])

    def blocks(order):
        return jnp.bitwise_xor(lax.axis_index("dp"), jnp.array(half_order(order), jnp.int32))

    packed = pack(table, query_rows, key_rows, value_rows)
    parts = [packed[0]] + [swap(packed[s], "head", group, s) for s in range(1, group)]
    pieces = split(out_grad, dp)
    nears = [swap(own, "head", group, 1) for own in pieces] if group == 4 else pieces
    both = join(pieces[0], nears[0], after=parts[1:])
    weights_full = lax.all_gather(out_weight, "dp", axis=0)

    tiles, counts = tile_index[0], tile_count[0]
    heads, cubes, slots = tiles.shape
    used = jnp.arange(slots, dtype=jnp.int32) < counts[:, :, None]
    listed = tiles[..., None] == jnp.arange(LANES, dtype=jnp.int32)
    allowed = jnp.any(listed & used[..., None], axis=2)
    bias = jnp.where(allowed, 0.0, masked_score).astype(BF16)
    bias = jnp.pad(bias, ((0, 0), (0, LANES - cubes), (0, 0)))

    att, att_t, weights, q_t, k, v = forward(table, token_order, bias, parts, after=[both])
    sums_to = widths[0] + widths[1]
    first = gather_rows(pieces[0], nears[0], group, both)
    grad = project(first, weights_full, 0, None, F32)
    state = outer(blocks(masks[0]), att_t, first, 0, sums_to)
    second = gather_rows(pieces[1], nears[1], group, join(pieces[1], nears[1], after=[att_t]))
    third = gather_rows(pieces[2], nears[2], group, None, held=[grad, state[0]])
    grad = project(second, weights_full, widths[0], grad, F32)
    state = outer(blocks(masks[0]), att_t, second, widths[0], sums_to, state)
    other = outer(blocks(masks[1]), att_t, third, 0, widths[2])
    grad = project(
        third, weights_full, widths[0] + widths[1], grad, BF16, after=[state[0], other[0]]
    )
    *back, keep, send, other_keep, other_send = backward(
        table, grad, att, weights, q_t, k, v, [*state, *other]
    )
    states = [(keep, send, masks[0]), (other_keep, other_send, masks[1])]
    while any(masks for _, _, masks in states):
        states = [fold(state, dp) for state in states]
    back = [back[0]] + [swap(back[s], "head", group, s) for s in range(1, group)]
    query_back, key_back, value_back = unpack(table, back)
    sums = [kept for kept, _, _ in states]
    return (att[None], query_back, key_back, value_back, jnp.concatenate(sums, axis=1))


def solution(mesh):
    placed = (
        P("dp", "head", None),
        P("dp", "head", None),
        P("dp", "head", None),
        P("dp", "head", None),
        P("head", "dp"),
        P("dp", None),
        P("dp", "head", None, None),
        P("dp", "head", None),
    )
    return jax.shard_map(
        functools.partial(local, mesh.shape["dp"], mesh.shape["head"]),
        mesh=mesh,
        in_specs=placed,
        out_specs=(
            P("dp", None, "head"),
            P("dp", "head", None),
            P("dp", "head", None),
            P("dp", "head", None),
            P("head", "dp"),
        ),
        check_vma=False,
    )
```

```python
import functools
import math

import jax
import jax.numpy as jnp
from jax import lax
from jax.experimental import pallas as pl
from jax.experimental.pallas import tpu as pltpu
from jax.sharding import PartitionSpec as P

HEAD_DIM = 128
CUBE_TOKENS = 128
LANES = 128

masked_score = -1e30
scale = 1.0 / math.sqrt(HEAD_DIM)
log2_e = math.log2(math.e)

BF16 = jnp.bfloat16
F32 = jnp.float32
NT = (((1,), (1,)), ((), ()))
NN = (((1,), (0,)), ((), ()))


def chunk_widths(columns):
    return [columns // 3] * 3


def light():
    return pl.CostEstimate(flops=1, bytes_accessed=1, transcendentals=0)


def whole(shape):
    return pl.BlockSpec(shape, lambda *_: (0,) * len(shape))


def awaited(after):
    return [pl.BlockSpec(memory_space=pl.ANY)] * len(after)


def dot(a, b, dims=NN):
    return lax.dot_general(a, b, dims, preferred_element_type=F32)


def params(limit_mib=60):
    return pltpu.CompilerParams(vmem_limit_bytes=limit_mib * 1024 * 1024)


def tables(group, here):
    partner = jnp.bitwise_xor(here, jnp.arange(group, dtype=jnp.int32))
    if group != 4:
        return jnp.concatenate([partner, partner, jnp.arange(group, dtype=jnp.int32)])
    middle = jnp.logical_or(here == 1, here == 2)
    slots = jnp.where(middle, jnp.array([0, 1, 3, 2], jnp.int32), jnp.arange(4, dtype=jnp.int32))
    return jnp.concatenate([partner, slots, jnp.bitwise_xor(here, slots)])


def slot(table, s):
    return table[table.shape[0] // 3 + s]


def owner(table, t):
    return table[table.shape[0] // 3 * 2 + t]


def pack_kernel(group, table, *refs):
    ins, outs = refs[: 3 * group], refs[-group:]
    for s, out in enumerate(outs):
        for i in range(3):
            out[i] = ins[3 * s + i][0]


def pack(table, q, k, v, after=()):
    group = table.shape[0] // 3
    rows, total = q.shape[1:]
    shape = (3, rows, total // group)
    in_specs = []
    for s in range(group):
        in_specs += [
            pl.BlockSpec((1, rows, total // group), lambda i, t, s=s: (0, 0, t[s]))
        ] * 3
    return pl.pallas_call(
        functools.partial(pack_kernel, group),
        out_shape=[jax.ShapeDtypeStruct(shape, BF16)] * group,
        grid_spec=pltpu.PrefetchScalarGridSpec(
            num_scalar_prefetch=1,
            grid=(1,),
            in_specs=in_specs + awaited(after),
            out_specs=[whole(shape)] * group,
        ),
        cost_estimate=light(),
        compiler_params=params(),
    )(table, *[q, k, v] * group, *after)


def split_kernel(dp, g_ref, *outs):
    columns = g_ref.shape[2] // dp
    before = 0
    for out in outs:
        part = out.shape[1] // dp
        for d in range(dp):
            start = d * columns + before
            out[:, d * part : (d + 1) * part] = g_ref[0, :, start : start + part]
        before += part


def split(g, dp):
    shapes = [(g.shape[1], width * dp) for width in chunk_widths(g.shape[2] // dp)]
    return pl.pallas_call(
        functools.partial(split_kernel, dp),
        out_shape=[jax.ShapeDtypeStruct(shape, BF16) for shape in shapes],
        grid=(1,),
        in_specs=[whole(g.shape)],
        out_specs=[whole(shape) for shape in shapes],
        cost_estimate=light(),
        compiler_params=params(),
    )(g)


def join_kernel(a_ref, b_ref, *refs):
    out = refs[-1]
    out[: a_ref.shape[0]] = a_ref[...]
    out[a_ref.shape[0] :] = b_ref[...]


def join(a, b, after=()):
    shape = (a.shape[0] + b.shape[0],) + a.shape[1:]
    return pl.pallas_call(
        join_kernel,
        out_shape=jax.ShapeDtypeStruct(shape, a.dtype),
        grid=(1,),
        in_specs=[whole(a.shape), whole(b.shape)] + awaited(after),
        out_specs=whole(shape),
        cost_estimate=light(),
        compiler_params=params(),
    )(a, b, *after)


def hold_kernel(*refs):
    pass


def hold(value, after):
    return pl.pallas_call(
        hold_kernel,
        out_shape=jax.ShapeDtypeStruct(value.shape, value.dtype),
        in_specs=awaited([value, *after]),
        out_specs=pl.BlockSpec(memory_space=pl.ANY),
        input_output_aliases={0: 0},
        cost_estimate=light(),
        compiler_params=params(),
    )(value, *after)


def unpack_first_kernel(partners, place, *refs):
    parts, outs = refs[: len(partners)], refs[-3:]
    width = parts[0].shape[2]
    for s, part in zip(partners, parts):
        columns = pl.ds(pl.multiple_of(place[s] * width, LANES), width)
        for i, out in enumerate(outs):
            out[0, :, columns] = part[i]


def unpack_last_kernel(count, place, *refs):
    for s, part in enumerate(refs[:count]):

        @pl.when(pl.program_id(0) == s)
        def _(part=part):
            for i, out in enumerate(refs[-3:]):
                out[0] = part[i]


def unpack(place, parts):
    group = place.shape[0] // 3
    _, rows, width = parts[0].shape
    shape = jax.ShapeDtypeStruct((1, rows, width * group), BF16)
    early = group // 2
    outs = pl.pallas_call(
        functools.partial(unpack_first_kernel, range(early)),
        out_shape=[shape] * 3,
        grid_spec=pltpu.PrefetchScalarGridSpec(
            num_scalar_prefetch=1,
            grid=(1,),
            in_specs=[whole(part.shape) for part in parts[:early]],
            out_specs=[whole(shape.shape)] * 3,
        ),
        cost_estimate=light(),
        compiler_params=params(),
    )(place, *parts[:early])
    late = parts[early:]
    return pl.pallas_call(
        functools.partial(unpack_last_kernel, len(late)),
        out_shape=[shape] * 3,
        grid_spec=pltpu.PrefetchScalarGridSpec(
            num_scalar_prefetch=1,
            grid=(len(late),),
            in_specs=[whole(part.shape) for part in late] + awaited(outs),
            out_specs=[pl.BlockSpec((1, rows, width), lambda i, t: (0, 0, t[early + i]))] * 3,
        ),
        input_output_aliases={1 + len(late) + i: i for i in range(3)},
        cost_estimate=light(),
        compiler_params=params(),
    )(place, *late, *outs)


def forward_kernel(group, table, order_ref, bias_ref, *refs):
    parts = refs[:group]
    att_ref, att_t_ref, weight_ref, q_t_ref, k_ref, v_ref, cube_ref, q_ref = refs[-8:]
    rows = parts[0].shape[1]
    total = q_ref.shape[0]

    @pl.when(pl.program_id(0) == 0)
    def _():
        position = lax.broadcasted_iota(jnp.int32, (total, LANES), 0)
        cube = lax.broadcasted_iota(jnp.int32, (total, LANES), 1)
        block = jnp.where(lax.div(position, CUBE_TOKENS) == cube, 1.0, 0.0).astype(BF16)
        for t in range(group):
            token = lax.broadcasted_iota(jnp.int32, (rows, total), 0) + owner(table, t) * rows
            onehot = jnp.where(token == order_ref[...], 1.0, 0.0).astype(BF16)
            cube_ref[t * rows : (t + 1) * rows, :] = dot(onehot, block).astype(BF16)

    for s, part in enumerate(parts):
        here = pl.ds(pl.multiple_of(slot(table, s) * rows, rows), rows)
        q_ref[here, :] = part[0]
        k_ref[here, :] = part[1]
        v_ref[here, :] = part[2]
    cubes = cube_ref[...]
    q, k, v = q_ref[...], k_ref[...], v_ref[...]
    bias = dot(cubes, bias_ref[0]).astype(BF16)
    scores = dot(
        jnp.concatenate([q, bias], axis=1), jnp.concatenate([k, cubes], axis=1), NT
    ) * (scale * log2_e)
    raised = jnp.exp2(scores - jnp.max(scores, axis=1, keepdims=True))
    weights = (raised * (1.0 / jnp.sum(raised, axis=1, keepdims=True))).astype(BF16)
    weight_ref[0] = weights
    output = dot(weights, v)
    for t in range(group):
        here = pl.ds(pl.multiple_of(owner(table, t) * rows, rows), rows)
        att_ref[here, :] = output[t * rows : (t + 1) * rows].astype(BF16)
    att_t_ref[...] = output.T.astype(BF16)
    q_t_ref[...] = q.astype(F32).T.astype(BF16)


def forward(table, order, bias, parts, after=()):
    group = len(parts)
    _, rows, width = parts[0].shape
    total = rows * group
    heads = width // HEAD_DIM
    column = pl.BlockSpec((total, HEAD_DIM), lambda h, *_: (0, h))
    row = pl.BlockSpec((HEAD_DIM, total), lambda h, *_: (h, 0))
    return pl.pallas_call(
        functools.partial(forward_kernel, group),
        out_shape=[
            jax.ShapeDtypeStruct((total, width), BF16),
            jax.ShapeDtypeStruct((width, total), BF16),
            jax.ShapeDtypeStruct((heads, total, total), BF16),
            jax.ShapeDtypeStruct((width, total), BF16),
            jax.ShapeDtypeStruct((total, width), BF16),
            jax.ShapeDtypeStruct((total, width), BF16),
        ],
        grid_spec=pltpu.PrefetchScalarGridSpec(
            num_scalar_prefetch=1,
            grid=(heads,),
            in_specs=[
                pl.BlockSpec((1, total), lambda h, *_: (0, 0)),
                pl.BlockSpec((1, LANES, LANES), lambda h, *_: (h, 0, 0)),
            ]
            + [pl.BlockSpec((3, rows, HEAD_DIM), lambda h, *_: (0, 0, h))] * group
            + awaited(after),
            out_specs=[
                column,
                row,
                pl.BlockSpec((1, total, total), lambda h, *_: (h, 0, 0)),
                row,
                column,
                column,
            ],
            scratch_shapes=[
                pltpu.VMEM((total, LANES), BF16),
                pltpu.VMEM((total, HEAD_DIM), BF16),
            ],
        ),
        cost_estimate=light(),
        compiler_params=params(),
    )(table, order, bias, *parts, *after)


def backward_kernel(
    group, chains, table, g_ref, att_ref, weight_ref, q_t_ref, k_ref, v_ref, *refs
):
    sums, refs = refs[: 2 * chains], refs[2 * chains :]
    outs, folded, held = refs[:group], refs[group:-1], refs[-1]
    rows = outs[0].shape[1]
    grad = g_ref[...]
    weights = weight_ref[0]
    grad_float = grad.astype(F32)
    att = jnp.concatenate(
        [
            att_ref[pl.ds(pl.multiple_of(owner(table, t) * rows, rows), rows), :]
            for t in range(group)
        ],
        axis=0,
    )
    delta = jnp.sum(grad_float * att.astype(F32), axis=1, keepdims=True)
    diff = (weights.astype(F32) * (dot(grad, v_ref[...], NT) - delta)).astype(BF16)
    held[0] = (dot(diff, k_ref[...]) * scale).astype(BF16)
    held[1] = (dot(q_t_ref[...], diff) * scale).T.astype(BF16)
    held[2] = dot(grad_float.T.astype(BF16), weights).T.astype(BF16)
    for s, out in enumerate(outs):
        here = pl.ds(pl.multiple_of(slot(table, s) * rows, rows), rows)
        out[...] = held[:, here, :]
    for c in range(chains):
        keep_ref, arrived_ref = sums[2 * c : 2 * c + 2]
        kept_ref, send_ref = folded[2 * c : 2 * c + 2]
        half = kept_ref.shape[0]
        kept_ref[...] = keep_ref[:half] + arrived_ref[:half]
        send_ref[...] = keep_ref[half:] + arrived_ref[half:]


def backward(table, grad, att, weights, q_t, k, v, sums):
    group = table.shape[0] // 3
    total, width = grad.shape
    rows = total // group
    heads = width // HEAD_DIM
    column = pl.BlockSpec((total, HEAD_DIM), lambda h, *_: (0, h))
    row = pl.BlockSpec((HEAD_DIM, total), lambda h, *_: (h, 0))
    sum_shapes, sum_specs, half_shapes, half_specs = [], [], [], []
    for keep, _ in sums:
        count, _, columns = keep.shape
        sum_specs += [pl.BlockSpec((count, HEAD_DIM, columns), lambda h, *_: (0, h, 0))] * 2
        half_specs += [pl.BlockSpec((count // 2, HEAD_DIM, columns), lambda h, *_: (0, h, 0))] * 2
        half_shapes += [jax.ShapeDtypeStruct((count // 2, width, columns), BF16)] * 2
    outs = pl.pallas_call(
        functools.partial(backward_kernel, group, len(sums)),
        out_shape=[jax.ShapeDtypeStruct((3, rows, width), BF16)] * group + half_shapes,
        grid_spec=pltpu.PrefetchScalarGridSpec(
            num_scalar_prefetch=1,
            grid=(heads,),
            in_specs=[
                column,
                column,
                pl.BlockSpec((1, total, total), lambda h, *_: (h, 0, 0)),
                row,
                column,
                column,
            ]
            + sum_specs,
            out_specs=[pl.BlockSpec((3, rows, HEAD_DIM), lambda h, *_: (0, 0, h))] * group
            + half_specs,
            scratch_shapes=[pltpu.VMEM((3, total, HEAD_DIM), BF16)],
        ),
        cost_estimate=light(),
        compiler_params=params(),
    )(table, grad, att, weights, q_t, k, v, *[x for pair in sums for x in pair])
    back, halves = outs[:group], outs[group:]
    return list(back), [halves[2 * c : 2 * c + 2] for c in range(len(sums))]


def block_rows(refs, columns):
    if len(refs) == 1:
        return refs[0][:, columns]
    own, near, inner, outer = refs
    return jnp.concatenate(
        [own[:, columns], near[:, columns], inner[:, columns] + outer[:, columns]], axis=0
    )


def block_columns(blocks, p, width):
    return pl.ds(pl.multiple_of(blocks[p] * width, LANES), width)


def project_kernel(count, pieces, first, *refs):
    weights, refs = refs[:pieces], refs[pieces:]
    rows, out = refs[:count], refs[-1]
    dp, _, unit = weights[0].shape
    part = unit * pieces
    total = None if first else refs[count][...]
    for p in range(dp):
        weight = jnp.concatenate([w[p] for w in weights], axis=1)
        term = dot(block_rows(rows, slice(p * part, (p + 1) * part)), weight, NT)
        total = term if total is None else total + term
    out[...] = total.astype(out.dtype)


def project(rows, weights, start, before, dtype, after=()):
    dp, heads, _ = weights.shape
    part = rows[0].shape[1] // dp
    unit = math.gcd(start, part)
    tokens = sum(r.shape[0] for r in rows[:3])
    before = [] if before is None else [before]
    at = range(start // unit, (start + part) // unit)
    return pl.pallas_call(
        functools.partial(project_kernel, len(rows), len(at), not before),
        out_shape=jax.ShapeDtypeStruct((tokens, heads), dtype),
        grid=(1,),
        in_specs=[pl.BlockSpec((dp, heads, unit), lambda i, c=c: (0, 0, c)) for c in at]
        + [whole(r.shape) for r in rows]
        + [whole(x.shape) for x in before]
        + awaited(after),
        out_specs=whole((tokens, heads)),
        cost_estimate=light(),
        compiler_params=params(),
    )(*[weights] * len(at), *rows, *before, *after)


def outer_kernel(count, start, passed, blocks, att_t_ref, *refs):
    rows = refs[:count]
    keep_ref, send_ref = refs[len(refs) - 2 - passed : len(refs) - passed]
    half, _, width = keep_ref.shape
    part = rows[0].shape[1] // (2 * half)
    att_t = att_t_ref[...]
    for p in range(2 * half):
        out = keep_ref if p < half else send_ref
        columns = pl.ds(pl.multiple_of(blocks[p] * part + start, LANES), width)
        out[p % half] = dot(att_t, block_rows(rows, columns)).astype(BF16)


def outer(blocks, att_t, rows, start, width, place, total, buffers=(), passed=()):
    half = blocks.shape[0] // 2
    heads = att_t.shape[0]
    first = 2 + len(rows)
    handed = list(buffers) + list(passed)
    outs = [jax.ShapeDtypeStruct((half, heads, total), BF16)] * 2
    aliases = {first + i: i for i in range(len(buffers))}
    aliases |= {first + len(buffers) + i: 2 + i for i in range(len(passed))}
    return pl.pallas_call(
        functools.partial(outer_kernel, len(rows), start, len(passed)),
        out_shape=outs + [jax.ShapeDtypeStruct(x.shape, x.dtype) for x in passed],
        grid_spec=pltpu.PrefetchScalarGridSpec(
            num_scalar_prefetch=1,
            grid=(1,),
            in_specs=[whole(att_t.shape)] + [whole(r.shape) for r in rows] + awaited(handed),
            out_specs=[pl.BlockSpec((half, heads, width), lambda i, b: (0, 0, place // width))] * 2
            + awaited(passed),
        ),
        input_output_aliases=aliases,
        cost_estimate=light(),
        compiler_params=params(),
    )(blocks, att_t, *rows, *handed)


def swap(value, axis, size, mask):
    return lax.ppermute(value, axis, [(i, i ^ mask) for i in range(size)])


def half_order(masks):
    order = [0]
    for mask in reversed(masks):
        order = order + [mask ^ r for r in order]
    return order


def fold(state, dp):
    kept, send, masks = state
    if not masks:
        return state
    kept = kept.astype(F32) + swap(send, "dp", dp, masks[0]).astype(F32)
    half = kept.shape[0] // 2
    if half == 0:
        kept = kept[0].astype(BF16)
        return kept, kept, masks[1:]
    return kept[:half], kept[half:].astype(BF16), masks[1:]


def gather_rows(own, near, group, both=None, held=()):
    if group != 4:
        return [lax.all_gather(own, "head", axis=0, tiled=True)]
    inner = lax.ppermute(join(own, near) if both is None else both, "head", [(1, 2), (2, 1)])
    if held:
        inner = hold(inner, held)
    outer = lax.ppermute(inner, "head", [(1, 0), (2, 3)])
    return [own, near, inner, outer]


def local(
    dp,
    group,
    query_rows,
    key_rows,
    value_rows,
    out_grad,
    out_weight,
    token_order,
    tile_index,
    tile_count,
):
    table = tables(group, lax.axis_index("head"))
    up = [1 << i for i in range(dp.bit_length() - 1)]
    masks = [up, up[:1] + up[:0:-1]]
    widths = chunk_widths(out_weight.shape[1])

    def blocks(order):
        return jnp.bitwise_xor(lax.axis_index("dp"), jnp.array(half_order(order), jnp.int32))

    packed = pack(table, query_rows, key_rows, value_rows)
    parts = [packed[0]] + [swap(packed[s], "head", group, s) for s in range(1, group)]
    pieces = split(out_grad, dp)
    nears = [swap(own, "head", group, 1) for own in pieces] if group == 4 else pieces
    both = join(pieces[0], nears[0], after=parts[1:])
    weights_full = lax.all_gather(out_weight, "dp", axis=0)

    tiles, counts = tile_index[0], tile_count[0]
    heads, cubes, slots = tiles.shape
    used = jnp.arange(slots, dtype=jnp.int32) < counts[:, :, None]
    listed = tiles[..., None] == jnp.arange(LANES, dtype=jnp.int32)
    allowed = jnp.any(listed & used[..., None], axis=2)
    bias = jnp.where(allowed, 0.0, masked_score).astype(BF16)
    bias = jnp.pad(bias, ((0, 0), (0, LANES - cubes), (0, 0)))

    att, att_t, weights, q_t, k, v = forward(table, token_order, bias, parts, after=[both])
    part = widths[0]
    cut = part // 2 if part % (2 * LANES) == 0 else 0
    order, other_order = blocks(masks[0]), blocks(masks[1])
    first = gather_rows(pieces[0], nears[0], group, both)
    grad = project(first, weights_full, 0, None, F32)
    state = outer(order, att_t, first, 0, part, 0, part + cut)
    second = gather_rows(pieces[1], nears[1], group, join(pieces[1], nears[1], after=[att_t]))
    third = gather_rows(pieces[2], nears[2], group, held=[grad, state[0]])
    grad = project(second, weights_full, part, grad, F32)
    if cut:
        state = outer(order, att_t, second, 0, cut, part, part + cut, state)
    rest = part - cut
    other = outer(other_order, att_t, second, cut, rest, part, part + rest)
    *other, keep, send, grad = outer(
        other_order, att_t, third, 0, part, 0, part + rest, other, passed=[*state, grad]
    )
    grad = project(third, weights_full, 2 * part, grad, BF16, after=[other[0], keep])
    arrived = swap(send, "dp", dp, masks[0][0])
    other_arrived = swap(other[1], "dp", dp, masks[1][0])
    back, halves = backward(
        table, grad, att, weights, q_t, k, v, [(keep, arrived), (other[0], other_arrived)]
    )
    states = [(*half, mask[1:]) for half, mask in zip(halves, masks)]
    while any(masks for _, _, masks in states):
        states = [fold(state, dp) for state in states]
    back = [back[0]] + [swap(back[s], "head", group, s) for s in range(1, group)]
    low, high = [kept for kept, _, _ in states]
    total = jnp.concatenate([low, high[:, part:], high[:, :part]], axis=1)
    query_back, key_back, value_back = unpack(table, back)
    return (att[None], query_back, key_back, value_back, total)


def solution(mesh):
    placed = (
        P("dp", "head", None),
        P("dp", "head", None),
        P("dp", "head", None),
        P("dp", "head", None),
        P("head", "dp"),
        P("dp", None),
        P("dp", "head", None, None),
        P("dp", "head", None),
    )
    return jax.shard_map(
        functools.partial(local, mesh.shape["dp"], mesh.shape["head"]),
        mesh=mesh,
        in_specs=placed,
        out_specs=(
            P("dp", None, "head"),
            P("dp", "head", None),
            P("dp", "head", None),
            P("dp", "head", None),
            P("head", "dp"),
        ),
        check_vma=False,
    )
```

```python
import functools
import math

import jax
import jax.numpy as jnp
from jax import lax
from jax.experimental import pallas as pl
from jax.experimental.pallas import tpu as pltpu
from jax.sharding import PartitionSpec as P

HEAD_DIM = 128
CUBE_TOKENS = 128
LANES = 128

masked_score = -1e30
scale = 1.0 / math.sqrt(HEAD_DIM)
log2_e = math.log2(math.e)

BF16 = jnp.bfloat16
F32 = jnp.float32
NT = (((1,), (1,)), ((), ()))
NN = (((1,), (0,)), ((), ()))


def chunk_widths(columns):
    return [columns // 3] * 3


def light():
    return pl.CostEstimate(flops=1, bytes_accessed=1, transcendentals=0)


def whole(shape):
    return pl.BlockSpec(shape, lambda *_: (0,) * len(shape))


def awaited(after):
    return [pl.BlockSpec(memory_space=pl.ANY)] * len(after)


def dot(a, b, dims=NN):
    return lax.dot_general(a, b, dims, preferred_element_type=F32)


def params(limit_mib=20):
    return pltpu.CompilerParams(vmem_limit_bytes=limit_mib * 1024 * 1024)


def tables(group, here):
    partner = jnp.bitwise_xor(here, jnp.arange(group, dtype=jnp.int32))
    if group != 4:
        return jnp.concatenate([partner, partner, jnp.arange(group, dtype=jnp.int32)])
    middle = jnp.logical_or(here == 1, here == 2)
    slots = jnp.where(middle, jnp.array([0, 1, 3, 2], jnp.int32), jnp.arange(4, dtype=jnp.int32))
    return jnp.concatenate([partner, slots, jnp.bitwise_xor(here, slots)])


def slot(table, s):
    return table[table.shape[0] // 3 + s]


def owner(table, t):
    return table[table.shape[0] // 3 * 2 + t]


def pack_kernel(group, table, *refs):
    ins, outs = refs[: 3 * group], refs[-group:]
    for s, out in enumerate(outs):
        for i in range(3):
            out[i] = ins[3 * s + i][0]


def pack(table, partners, q, k, v, after=()):
    group = table.shape[0] // 3
    rows, total = q.shape[1:]
    shape = (3, rows, total // group)
    in_specs = []
    for s in partners:
        in_specs += [
            pl.BlockSpec((1, rows, total // group), lambda i, t, s=s: (0, 0, t[s]))
        ] * 3
    return pl.pallas_call(
        functools.partial(pack_kernel, len(partners)),
        out_shape=[jax.ShapeDtypeStruct(shape, BF16)] * len(partners),
        grid_spec=pltpu.PrefetchScalarGridSpec(
            num_scalar_prefetch=1,
            grid=(1,),
            in_specs=in_specs + awaited(after),
            out_specs=[whole(shape)] * len(partners),
        ),
        cost_estimate=light(),
        compiler_params=params(),
    )(table, *[q, k, v] * len(partners), *after)


def split_kernel(dp, g_ref, *outs):
    columns = g_ref.shape[2] // dp
    before = 0
    for out in outs:
        part = out.shape[1] // dp
        for d in range(dp):
            start = d * columns + before
            out[:, d * part : (d + 1) * part] = g_ref[0, :, start : start + part]
        before += part


def split(g, dp):
    shapes = [(g.shape[1], width * dp) for width in chunk_widths(g.shape[2] // dp)]
    return pl.pallas_call(
        functools.partial(split_kernel, dp),
        out_shape=[jax.ShapeDtypeStruct(shape, BF16) for shape in shapes],
        grid=(1,),
        in_specs=[whole(g.shape)],
        out_specs=[whole(shape) for shape in shapes],
        cost_estimate=light(),
        compiler_params=params(),
    )(g)


def join_kernel(a_ref, b_ref, *refs):
    out = refs[-1]
    out[: a_ref.shape[0]] = a_ref[...]
    out[a_ref.shape[0] :] = b_ref[...]


def join(a, b, after=()):
    shape = (a.shape[0] + b.shape[0],) + a.shape[1:]
    return pl.pallas_call(
        join_kernel,
        out_shape=jax.ShapeDtypeStruct(shape, a.dtype),
        grid=(1,),
        in_specs=[whole(a.shape), whole(b.shape)] + awaited(after),
        out_specs=whole(shape),
        cost_estimate=light(),
        compiler_params=params(),
    )(a, b, *after)


def hold_kernel(*refs):
    pass


def hold(value, after):
    return pl.pallas_call(
        hold_kernel,
        out_shape=jax.ShapeDtypeStruct(value.shape, value.dtype),
        in_specs=awaited([value, *after]),
        out_specs=pl.BlockSpec(memory_space=pl.ANY),
        input_output_aliases={0: 0},
        cost_estimate=light(),
        compiler_params=params(),
    )(value, *after)


def unpack_first_kernel(partners, place, *refs):
    parts, outs = refs[: len(partners)], refs[-3:]
    width = parts[0].shape[2]
    for s, part in zip(partners, parts):
        columns = pl.ds(pl.multiple_of(place[s] * width, LANES), width)
        for i, out in enumerate(outs):
            out[0, :, columns] = part[i]


def unpack_last_kernel(count, place, *refs):
    for s, part in enumerate(refs[:count]):

        @pl.when(pl.program_id(0) == s)
        def _(part=part):
            for i, out in enumerate(refs[-3:]):
                out[0] = part[i]


def unpack(place, parts):
    group = place.shape[0] // 3
    _, rows, width = parts[0].shape
    shape = jax.ShapeDtypeStruct((1, rows, width * group), BF16)
    early = group // 2
    outs = pl.pallas_call(
        functools.partial(unpack_first_kernel, range(early)),
        out_shape=[shape] * 3,
        grid_spec=pltpu.PrefetchScalarGridSpec(
            num_scalar_prefetch=1,
            grid=(1,),
            in_specs=[whole(part.shape) for part in parts[:early]],
            out_specs=[whole(shape.shape)] * 3,
        ),
        cost_estimate=light(),
        compiler_params=params(),
    )(place, *parts[:early])
    late = parts[early:]
    return pl.pallas_call(
        functools.partial(unpack_last_kernel, len(late)),
        out_shape=[shape] * 3,
        grid_spec=pltpu.PrefetchScalarGridSpec(
            num_scalar_prefetch=1,
            grid=(len(late),),
            in_specs=[whole(part.shape) for part in late] + awaited(outs),
            out_specs=[pl.BlockSpec((1, rows, width), lambda i, t: (0, 0, t[early + i]))] * 3,
        ),
        input_output_aliases={1 + len(late) + i: i for i in range(3)},
        cost_estimate=light(),
        compiler_params=params(),
    )(place, *late, *outs)


def forward_kernel(group, table, order_ref, bias_ref, *refs):
    parts = refs[:group]
    att_ref, att_t_ref, weight_ref, q_t_ref, k_ref, v_ref, cube_ref, q_ref = refs[-8:]
    rows = parts[0].shape[1]
    total = q_ref.shape[0]

    @pl.when(pl.program_id(0) == 0)
    def _():
        position = lax.broadcasted_iota(jnp.int32, (total, LANES), 0)
        cube = lax.broadcasted_iota(jnp.int32, (total, LANES), 1)
        block = jnp.where(lax.div(position, CUBE_TOKENS) == cube, 1.0, 0.0).astype(BF16)
        for t in range(group):
            token = lax.broadcasted_iota(jnp.int32, (rows, total), 0) + owner(table, t) * rows
            onehot = jnp.where(token == order_ref[...], 1.0, 0.0).astype(BF16)
            cube_ref[t * rows : (t + 1) * rows, :] = dot(onehot, block).astype(BF16)

    for s, part in enumerate(parts):
        here = pl.ds(pl.multiple_of(slot(table, s) * rows, rows), rows)
        q_ref[here, :] = part[0]
        k_ref[here, :] = part[1]
        v_ref[here, :] = part[2]
    cubes = cube_ref[...]
    q, k, v = q_ref[...], k_ref[...], v_ref[...]
    bias = dot(cubes, bias_ref[0]).astype(BF16)
    scores = dot(
        jnp.concatenate([q, bias], axis=1), jnp.concatenate([k, cubes], axis=1), NT
    ) * (scale * log2_e)
    raised = jnp.exp2(scores - jnp.max(scores, axis=1, keepdims=True))
    weights = (raised * (1.0 / jnp.sum(raised, axis=1, keepdims=True))).astype(BF16)
    weight_ref[0] = weights
    output = dot(weights, v)
    for t in range(group):
        here = pl.ds(pl.multiple_of(owner(table, t) * rows, rows), rows)
        att_ref[here, :] = output[t * rows : (t + 1) * rows].astype(BF16)
    att_t_ref[...] = output.T.astype(BF16)
    q_t_ref[...] = q.astype(F32).T.astype(BF16)


def forward(table, order, bias, parts, after=()):
    group = len(parts)
    _, rows, width = parts[0].shape
    total = rows * group
    heads = width // HEAD_DIM
    column = pl.BlockSpec((total, HEAD_DIM), lambda h, *_: (0, h))
    row = pl.BlockSpec((HEAD_DIM, total), lambda h, *_: (h, 0))
    return pl.pallas_call(
        functools.partial(forward_kernel, group),
        out_shape=[
            jax.ShapeDtypeStruct((total, width), BF16),
            jax.ShapeDtypeStruct((width, total), BF16),
            jax.ShapeDtypeStruct((heads, total, total), BF16),
            jax.ShapeDtypeStruct((width, total), BF16),
            jax.ShapeDtypeStruct((total, width), BF16),
            jax.ShapeDtypeStruct((total, width), BF16),
        ],
        grid_spec=pltpu.PrefetchScalarGridSpec(
            num_scalar_prefetch=1,
            grid=(heads,),
            in_specs=[
                pl.BlockSpec((1, total), lambda h, *_: (0, 0)),
                pl.BlockSpec((1, LANES, LANES), lambda h, *_: (h, 0, 0)),
            ]
            + [pl.BlockSpec((3, rows, HEAD_DIM), lambda h, *_: (0, 0, h))] * group
            + awaited(after),
            out_specs=[
                column,
                row,
                pl.BlockSpec((1, total, total), lambda h, *_: (h, 0, 0)),
                row,
                column,
                column,
            ],
            scratch_shapes=[
                pltpu.VMEM((total, LANES), BF16),
                pltpu.VMEM((total, HEAD_DIM), BF16),
            ],
        ),
        cost_estimate=light(),
        compiler_params=params(),
    )(table, order, bias, *parts, *after)


def backward_kernel(
    group, chains, table, g_ref, att_ref, weight_ref, q_t_ref, k_ref, v_ref, *refs
):
    sums, refs = refs[: 2 * chains], refs[2 * chains :]
    outs, folded, held = refs[:group], refs[group:-1], refs[-1]
    rows = outs[0].shape[1]
    grad = g_ref[...]
    weights = weight_ref[0]
    grad_float = grad.astype(F32)
    att = jnp.concatenate(
        [
            att_ref[pl.ds(pl.multiple_of(owner(table, t) * rows, rows), rows), :]
            for t in range(group)
        ],
        axis=0,
    )
    delta = jnp.sum(grad_float * att.astype(F32), axis=1, keepdims=True)
    diff = (weights.astype(F32) * (dot(grad, v_ref[...], NT) - delta)).astype(BF16)
    held[0] = (dot(diff, k_ref[...]) * scale).astype(BF16)
    held[1] = (dot(q_t_ref[...], diff) * scale).T.astype(BF16)
    held[2] = dot(grad_float.T.astype(BF16), weights).T.astype(BF16)
    for s, out in enumerate(outs):
        here = pl.ds(pl.multiple_of(slot(table, s) * rows, rows), rows)
        out[...] = held[:, here, :]
    for c in range(chains):
        keep_ref, arrived_ref = sums[2 * c : 2 * c + 2]
        kept_ref, send_ref = folded[2 * c : 2 * c + 2]
        half = kept_ref.shape[0]
        kept_ref[...] = keep_ref[:half] + arrived_ref[:half]
        send_ref[...] = keep_ref[half:] + arrived_ref[half:]


def backward(table, grad, att, weights, q_t, k, v, sums):
    group = table.shape[0] // 3
    total, width = grad.shape
    rows = total // group
    heads = width // HEAD_DIM
    column = pl.BlockSpec((total, HEAD_DIM), lambda h, *_: (0, h))
    row = pl.BlockSpec((HEAD_DIM, total), lambda h, *_: (h, 0))
    sum_shapes, sum_specs, half_shapes, half_specs = [], [], [], []
    for keep, _ in sums:
        count, _, columns = keep.shape
        sum_specs += [pl.BlockSpec((count, HEAD_DIM, columns), lambda h, *_: (0, h, 0))] * 2
        half_specs += [pl.BlockSpec((count // 2, HEAD_DIM, columns), lambda h, *_: (0, h, 0))] * 2
        half_shapes += [jax.ShapeDtypeStruct((count // 2, width, columns), BF16)] * 2
    outs = pl.pallas_call(
        functools.partial(backward_kernel, group, len(sums)),
        out_shape=[jax.ShapeDtypeStruct((3, rows, width), BF16)] * group + half_shapes,
        grid_spec=pltpu.PrefetchScalarGridSpec(
            num_scalar_prefetch=1,
            grid=(heads,),
            in_specs=[
                column,
                column,
                pl.BlockSpec((1, total, total), lambda h, *_: (h, 0, 0)),
                row,
                column,
                column,
            ]
            + sum_specs,
            out_specs=[pl.BlockSpec((3, rows, HEAD_DIM), lambda h, *_: (0, 0, h))] * group
            + half_specs,
            scratch_shapes=[pltpu.VMEM((3, total, HEAD_DIM), BF16)],
        ),
        cost_estimate=light(),
        compiler_params=params(),
    )(table, grad, att, weights, q_t, k, v, *[x for pair in sums for x in pair])
    back, halves = outs[:group], outs[group:]
    return list(back), [halves[2 * c : 2 * c + 2] for c in range(len(sums))]


def block_rows(refs, columns):
    if len(refs) == 1:
        return refs[0][:, columns]
    own, near, inner, outer = refs
    return jnp.concatenate(
        [own[:, columns], near[:, columns], inner[:, columns] + outer[:, columns]], axis=0
    )


def block_columns(blocks, p, width):
    return pl.ds(pl.multiple_of(blocks[p] * width, LANES), width)


def project_kernel(count, pieces, first, *refs):
    weights, refs = refs[:pieces], refs[pieces:]
    rows, out = refs[:count], refs[-1]
    dp, _, unit = weights[0].shape
    part = unit * pieces
    total = None if first else refs[count][...]
    for p in range(dp):
        weight = jnp.concatenate([w[p] for w in weights], axis=1)
        term = dot(block_rows(rows, slice(p * part, (p + 1) * part)), weight, NT)
        total = term if total is None else total + term
    out[...] = total.astype(out.dtype)


def project(rows, weights, start, before, dtype, after=()):
    dp, heads, _ = weights.shape
    part = rows[0].shape[1] // dp
    unit = math.gcd(start, part)
    tokens = sum(r.shape[0] for r in rows[:3])
    before = [] if before is None else [before]
    at = range(start // unit, (start + part) // unit)
    return pl.pallas_call(
        functools.partial(project_kernel, len(rows), len(at), not before),
        out_shape=jax.ShapeDtypeStruct((tokens, heads), dtype),
        grid=(1,),
        in_specs=[pl.BlockSpec((dp, heads, unit), lambda i, c=c: (0, 0, c)) for c in at]
        + [whole(r.shape) for r in rows]
        + [whole(x.shape) for x in before]
        + awaited(after),
        out_specs=whole((tokens, heads)),
        cost_estimate=light(),
        compiler_params=params(),
    )(*[weights] * len(at), *rows, *before, *after)


def outer_kernel(count, start, passed, blocks, att_t_ref, *refs):
    rows = refs[:count]
    keep_ref, send_ref = refs[len(refs) - 2 - passed : len(refs) - passed]
    half, _, width = keep_ref.shape
    part = rows[0].shape[1] // (2 * half)
    att_t = att_t_ref[...]
    for p in range(2 * half):
        out = keep_ref if p < half else send_ref
        columns = pl.ds(pl.multiple_of(blocks[p] * part + start, LANES), width)
        out[p % half] = dot(att_t, block_rows(rows, columns)).astype(BF16)


def outer(blocks, att_t, rows, start, width, place, total, buffers=(), passed=()):
    half = blocks.shape[0] // 2
    heads = att_t.shape[0]
    first = 2 + len(rows)
    handed = list(buffers) + list(passed)
    outs = [jax.ShapeDtypeStruct((half, heads, total), BF16)] * 2
    aliases = {first + i: i for i in range(len(buffers))}
    aliases |= {first + len(buffers) + i: 2 + i for i in range(len(passed))}
    return pl.pallas_call(
        functools.partial(outer_kernel, len(rows), start, len(passed)),
        out_shape=outs + [jax.ShapeDtypeStruct(x.shape, x.dtype) for x in passed],
        grid_spec=pltpu.PrefetchScalarGridSpec(
            num_scalar_prefetch=1,
            grid=(1,),
            in_specs=[whole(att_t.shape)] + [whole(r.shape) for r in rows] + awaited(handed),
            out_specs=[pl.BlockSpec((half, heads, width), lambda i, b: (0, 0, place // width))] * 2
            + awaited(passed),
        ),
        input_output_aliases=aliases,
        cost_estimate=light(),
        compiler_params=params(),
    )(blocks, att_t, *rows, *handed)


def swap(value, axis, size, mask):
    return lax.ppermute(value, axis, [(i, i ^ mask) for i in range(size)])


def half_order(masks):
    order = [0]
    for mask in reversed(masks):
        order = order + [mask ^ r for r in order]
    return order


def fold(state, dp):
    kept, send, masks = state
    if not masks:
        return state
    kept = kept.astype(F32) + swap(send, "dp", dp, masks[0]).astype(F32)
    half = kept.shape[0] // 2
    if half == 0:
        return kept[0], kept[0], masks[1:]
    return kept[:half], kept[half:].astype(BF16), masks[1:]


def gather_rows(own, near, group, both=None, held=()):
    if group != 4:
        return [lax.all_gather(own, "head", axis=0, tiled=True)]
    inner = lax.ppermute(join(own, near) if both is None else both, "head", [(1, 2), (2, 1)])
    if held:
        inner = hold(inner, held)
    outer = lax.ppermute(inner, "head", [(1, 0), (2, 3)])
    return [own, near, inner, outer]


def local(
    dp,
    group,
    query_rows,
    key_rows,
    value_rows,
    out_grad,
    out_weight,
    token_order,
    tile_index,
    tile_count,
):
    table = tables(group, lax.axis_index("head"))
    up = [1 << i for i in range(dp.bit_length() - 1)]
    masks = [up, up[:1] + up[:0:-1]]
    widths = chunk_widths(out_weight.shape[1])

    def blocks(order):
        return jnp.bitwise_xor(lax.axis_index("dp"), jnp.array(half_order(order), jnp.int32))

    arrays = (query_rows, key_rows, value_rows)
    packed = pack(table, range(1, group), *arrays)
    parts = [swap(rows, "head", group, 1 + i) for i, rows in enumerate(packed)]
    parts = list(pack(table, [0], *arrays, after=parts[:1])) + parts
    pieces = split(out_grad, dp)
    nears = [swap(own, "head", group, 1) for own in pieces] if group == 4 else pieces
    both = join(pieces[0], nears[0], after=parts[1:])
    weights_full = lax.all_gather(out_weight, "dp", axis=0)

    tiles, counts = tile_index[0], tile_count[0]
    heads, cubes, slots = tiles.shape
    used = jnp.arange(slots, dtype=jnp.int32) < counts[:, :, None]
    listed = tiles[..., None] == jnp.arange(LANES, dtype=jnp.int32)
    allowed = jnp.any(listed & used[..., None], axis=2)
    bias = jnp.where(allowed, 0.0, masked_score).astype(BF16)
    bias = jnp.pad(bias, ((0, 0), (0, LANES - cubes), (0, 0)))

    att, att_t, weights, q_t, k, v = forward(table, token_order, bias, parts, after=[both])
    part = widths[0]
    cut = part // 2 if part % (2 * LANES) == 0 else 0
    order, other_order = blocks(masks[0]), blocks(masks[1])
    first = gather_rows(pieces[0], nears[0], group, both)
    grad = project(first, weights_full, 0, None, F32)
    state = outer(order, att_t, first, 0, part, 0, part + cut)
    second = gather_rows(pieces[1], nears[1], group, join(pieces[1], nears[1], after=[att_t]))
    third = gather_rows(pieces[2], nears[2], group, held=[grad, state[0]])
    grad = project(second, weights_full, part, grad, F32)
    if cut:
        state = outer(order, att_t, second, 0, cut, part, part + cut, state)
    rest = part - cut
    other = outer(other_order, att_t, second, cut, rest, part, part + rest)
    *other, keep, send, grad = outer(
        other_order, att_t, third, 0, part, 0, part + rest, other, passed=[*state, grad]
    )
    grad = project(third, weights_full, 2 * part, grad, BF16, after=[other[0], keep])
    arrived = swap(send, "dp", dp, masks[0][0])
    other_arrived = swap(other[1], "dp", dp, masks[1][0])
    back, halves = backward(
        table, grad, att, weights, q_t, k, v, [(keep, arrived), (other[0], other_arrived)]
    )
    states = [(*half, mask[1:]) for half, mask in zip(halves, masks)]
    while any(masks for _, _, masks in states):
        states = [fold(state, dp) for state in states]
    back = [back[0]] + [swap(back[s], "head", group, s) for s in range(1, group)]
    low, high = [kept for kept, _, _ in states]
    total = jnp.concatenate([low, high[:, part:], high[:, :part]], axis=1).astype(BF16)
    query_back, key_back, value_back = unpack(table, back)
    return (att[None], query_back, key_back, value_back, total)


def solution(mesh):
    placed = (
        P("dp", "head", None),
        P("dp", "head", None),
        P("dp", "head", None),
        P("dp", "head", None),
        P("head", "dp"),
        P("dp", None),
        P("dp", "head", None, None),
        P("dp", "head", None),
    )
    return jax.shard_map(
        functools.partial(local, mesh.shape["dp"], mesh.shape["head"]),
        mesh=mesh,
        in_specs=placed,
        out_specs=(
            P("dp", None, "head"),
            P("dp", "head", None),
            P("dp", "head", None),
            P("dp", "head", None),
            P("head", "dp"),
        ),
        check_vma=False,
    )
```

```python
import functools
import math

import jax
import jax.numpy as jnp
from jax import lax
from jax.experimental import pallas as pl
from jax.experimental.pallas import tpu as pltpu
from jax.sharding import PartitionSpec as P

HEAD_DIM = 128
CUBE_TOKENS = 128
LANES = 128

masked_score = -1e30
scale = 1.0 / math.sqrt(HEAD_DIM)
log2_e = math.log2(math.e)

BF16 = jnp.bfloat16
F32 = jnp.float32
NT = (((1,), (1,)), ((), ()))
NN = (((1,), (0,)), ((), ()))


def chunk_widths(columns):
    return [columns // 3] * 3


def light():
    return pl.CostEstimate(flops=1, bytes_accessed=1, transcendentals=0)


def whole(shape):
    return pl.BlockSpec(shape, lambda *_: (0,) * len(shape))


def awaited(after):
    return [pl.BlockSpec(memory_space=pl.ANY)] * len(after)


def dot(a, b, dims=NN):
    return lax.dot_general(a, b, dims, preferred_element_type=F32)


def params(limit_mib=20):
    return pltpu.CompilerParams(vmem_limit_bytes=limit_mib * 1024 * 1024)


def tables(group, here):
    partner = jnp.bitwise_xor(here, jnp.arange(group, dtype=jnp.int32))
    if group != 4:
        return jnp.concatenate([partner, partner, jnp.arange(group, dtype=jnp.int32)])
    middle = jnp.logical_or(here == 1, here == 2)
    slots = jnp.where(middle, jnp.array([0, 1, 3, 2], jnp.int32), jnp.arange(4, dtype=jnp.int32))
    return jnp.concatenate([partner, slots, jnp.bitwise_xor(here, slots)])


def slot(table, s):
    return table[table.shape[0] // 3 + s]


def owner(table, t):
    return table[table.shape[0] // 3 * 2 + t]


def pack_kernel(group, table, *refs):
    ins, outs = refs[: 3 * group], refs[-group:]
    for s, out in enumerate(outs):
        for i in range(3):
            out[i] = ins[3 * s + i][0]


def pack(table, partners, q, k, v, after=()):
    group = table.shape[0] // 3
    rows, total = q.shape[1:]
    shape = (3, rows, total // group)
    in_specs = []
    for s in partners:
        in_specs += [
            pl.BlockSpec((1, rows, total // group), lambda i, t, s=s: (0, 0, t[s]))
        ] * 3
    return pl.pallas_call(
        functools.partial(pack_kernel, len(partners)),
        out_shape=[jax.ShapeDtypeStruct(shape, BF16)] * len(partners),
        grid_spec=pltpu.PrefetchScalarGridSpec(
            num_scalar_prefetch=1,
            grid=(1,),
            in_specs=in_specs + awaited(after),
            out_specs=[whole(shape)] * len(partners),
        ),
        cost_estimate=light(),
        compiler_params=params(60),
    )(table, *[q, k, v] * len(partners), *after)


def split_kernel(dp, g_ref, *outs):
    columns = g_ref.shape[2] // dp
    before = 0
    for out in outs:
        part = out.shape[1] // dp
        for d in range(dp):
            start = d * columns + before
            out[:, d * part : (d + 1) * part] = g_ref[0, :, start : start + part]
        before += part


def split(g, dp):
    shapes = [(g.shape[1], width * dp) for width in chunk_widths(g.shape[2] // dp)]
    return pl.pallas_call(
        functools.partial(split_kernel, dp),
        out_shape=[jax.ShapeDtypeStruct(shape, BF16) for shape in shapes],
        grid=(1,),
        in_specs=[whole(g.shape)],
        out_specs=[whole(shape) for shape in shapes],
        cost_estimate=light(),
        compiler_params=params(),
    )(g)


def join_kernel(a_ref, b_ref, *refs):
    out = refs[-1]
    out[: a_ref.shape[0]] = a_ref[...]
    out[a_ref.shape[0] :] = b_ref[...]


def join(a, b, after=()):
    shape = (a.shape[0] + b.shape[0],) + a.shape[1:]
    return pl.pallas_call(
        join_kernel,
        out_shape=jax.ShapeDtypeStruct(shape, a.dtype),
        grid=(1,),
        in_specs=[whole(a.shape), whole(b.shape)] + awaited(after),
        out_specs=whole(shape),
        cost_estimate=light(),
        compiler_params=params(),
    )(a, b, *after)


def hold_kernel(*refs):
    pass


def hold(value, after):
    return pl.pallas_call(
        hold_kernel,
        out_shape=jax.ShapeDtypeStruct(value.shape, value.dtype),
        in_specs=awaited([value, *after]),
        out_specs=pl.BlockSpec(memory_space=pl.ANY),
        input_output_aliases={0: 0},
        cost_estimate=light(),
        compiler_params=params(),
    )(value, *after)


def unpack_first_kernel(partners, place, *refs):
    parts, outs = refs[: len(partners)], refs[-3:]
    width = parts[0].shape[2]
    for s, part in zip(partners, parts):
        columns = pl.ds(pl.multiple_of(place[s] * width, LANES), width)
        for i, out in enumerate(outs):
            out[0, :, columns] = part[i]


def unpack_last_kernel(count, place, *refs):
    for s, part in enumerate(refs[:count]):

        @pl.when(pl.program_id(0) == s)
        def _(part=part):
            for i, out in enumerate(refs[-3:]):
                out[0] = part[i]


def unpack(place, parts):
    group = place.shape[0] // 3
    _, rows, width = parts[0].shape
    shape = jax.ShapeDtypeStruct((1, rows, width * group), BF16)
    early = group // 2
    outs = pl.pallas_call(
        functools.partial(unpack_first_kernel, range(early)),
        out_shape=[shape] * 3,
        grid_spec=pltpu.PrefetchScalarGridSpec(
            num_scalar_prefetch=1,
            grid=(1,),
            in_specs=[whole(part.shape) for part in parts[:early]],
            out_specs=[whole(shape.shape)] * 3,
        ),
        cost_estimate=light(),
        compiler_params=params(),
    )(place, *parts[:early])
    late = parts[early:]
    return pl.pallas_call(
        functools.partial(unpack_last_kernel, len(late)),
        out_shape=[shape] * 3,
        grid_spec=pltpu.PrefetchScalarGridSpec(
            num_scalar_prefetch=1,
            grid=(len(late),),
            in_specs=[whole(part.shape) for part in late] + awaited(outs),
            out_specs=[pl.BlockSpec((1, rows, width), lambda i, t: (0, 0, t[early + i]))] * 3,
        ),
        input_output_aliases={1 + len(late) + i: i for i in range(3)},
        cost_estimate=light(),
        compiler_params=params(),
    )(place, *late, *outs)


def forward_kernel(group, table, order_ref, bias_ref, *refs):
    parts = refs[:group]
    att_ref, att_t_ref, weight_ref, q_t_ref, k_ref, v_ref, cube_ref, q_ref = refs[-8:]
    rows = parts[0].shape[1]
    total = q_ref.shape[0]

    @pl.when(pl.program_id(0) == 0)
    def _():
        position = lax.broadcasted_iota(jnp.int32, (total, LANES), 0)
        cube = lax.broadcasted_iota(jnp.int32, (total, LANES), 1)
        block = jnp.where(lax.div(position, CUBE_TOKENS) == cube, 1.0, 0.0).astype(BF16)
        for t in range(group):
            token = lax.broadcasted_iota(jnp.int32, (rows, total), 0) + owner(table, t) * rows
            onehot = jnp.where(token == order_ref[...], 1.0, 0.0).astype(BF16)
            cube_ref[t * rows : (t + 1) * rows, :] = dot(onehot, block).astype(BF16)

    for s, part in enumerate(parts):
        here = pl.ds(pl.multiple_of(slot(table, s) * rows, rows), rows)
        q_ref[here, :] = part[0]
        k_ref[here, :] = part[1]
        v_ref[here, :] = part[2]
    cubes = cube_ref[...]
    q, k, v = q_ref[...], k_ref[...], v_ref[...]
    bias = dot(cubes, bias_ref[0]).astype(BF16)
    scores = dot(
        jnp.concatenate([q, bias], axis=1), jnp.concatenate([k, cubes], axis=1), NT
    ) * (scale * log2_e)
    raised = jnp.exp2(scores - jnp.max(scores, axis=1, keepdims=True))
    weights = (raised * (1.0 / jnp.sum(raised, axis=1, keepdims=True))).astype(BF16)
    weight_ref[0] = weights
    output = dot(weights, v)
    for t in range(group):
        here = pl.ds(pl.multiple_of(owner(table, t) * rows, rows), rows)
        att_ref[here, :] = output[t * rows : (t + 1) * rows].astype(BF16)
    att_t_ref[...] = output.T.astype(BF16)
    q_t_ref[...] = q.astype(F32).T.astype(BF16)


def forward(table, order, bias, parts, after=()):
    group = len(parts)
    _, rows, width = parts[0].shape
    total = rows * group
    heads = width // HEAD_DIM
    column = pl.BlockSpec((total, HEAD_DIM), lambda h, *_: (0, h))
    row = pl.BlockSpec((HEAD_DIM, total), lambda h, *_: (h, 0))
    return pl.pallas_call(
        functools.partial(forward_kernel, group),
        out_shape=[
            jax.ShapeDtypeStruct((total, width), BF16),
            jax.ShapeDtypeStruct((width, total), BF16),
            jax.ShapeDtypeStruct((heads, total, total), BF16),
            jax.ShapeDtypeStruct((width, total), BF16),
            jax.ShapeDtypeStruct((total, width), BF16),
            jax.ShapeDtypeStruct((total, width), BF16),
        ],
        grid_spec=pltpu.PrefetchScalarGridSpec(
            num_scalar_prefetch=1,
            grid=(heads,),
            in_specs=[
                pl.BlockSpec((1, total), lambda h, *_: (0, 0)),
                pl.BlockSpec((1, LANES, LANES), lambda h, *_: (h, 0, 0)),
            ]
            + [pl.BlockSpec((3, rows, HEAD_DIM), lambda h, *_: (0, 0, h))] * group
            + awaited(after),
            out_specs=[
                column,
                row,
                pl.BlockSpec((1, total, total), lambda h, *_: (h, 0, 0)),
                row,
                column,
                column,
            ],
            scratch_shapes=[
                pltpu.VMEM((total, LANES), BF16),
                pltpu.VMEM((total, HEAD_DIM), BF16),
            ],
        ),
        cost_estimate=light(),
        compiler_params=params(),
    )(table, order, bias, *parts, *after)


def backward_kernel(
    group, chains, table, g_ref, att_ref, weight_ref, q_t_ref, k_ref, v_ref, *refs
):
    sums, refs = refs[: 2 * chains], refs[2 * chains :]
    outs, folded, held = refs[:group], refs[group:-1], refs[-1]
    rows = outs[0].shape[1]
    for i in range(weight_ref.shape[0]):
        one = slice(i * HEAD_DIM, (i + 1) * HEAD_DIM)
        grad = g_ref[:, one]
        weights = weight_ref[i]
        grad_float = grad.astype(F32)
        att = jnp.concatenate(
            [
                att_ref[pl.ds(pl.multiple_of(owner(table, t) * rows, rows), rows), one]
                for t in range(group)
            ],
            axis=0,
        )
        delta = jnp.sum(grad_float * att.astype(F32), axis=1, keepdims=True)
        diff = (weights.astype(F32) * (dot(grad, v_ref[:, one], NT) - delta)).astype(BF16)
        held[0, :, one] = (dot(diff, k_ref[:, one]) * scale).astype(BF16)
        held[1, :, one] = (dot(q_t_ref[one, :], diff) * scale).T.astype(BF16)
        held[2, :, one] = dot(grad_float.T.astype(BF16), weights).T.astype(BF16)
    for s, out in enumerate(outs):
        here = pl.ds(pl.multiple_of(slot(table, s) * rows, rows), rows)
        out[...] = held[:, here, :]
    for c in range(chains):
        keep_ref, arrived_ref = sums[2 * c : 2 * c + 2]
        kept_ref, send_ref = folded[2 * c : 2 * c + 2]
        half = kept_ref.shape[0]
        kept_ref[...] = keep_ref[:half] + arrived_ref[:half]
        send_ref[...] = keep_ref[half:] + arrived_ref[half:]


def backward(table, grad, att, weights, q_t, k, v, sums):
    group = table.shape[0] // 3
    total, width = grad.shape
    rows = total // group
    heads = width // HEAD_DIM
    per = 2 if heads % 2 == 0 else 1
    wide = per * HEAD_DIM
    column = pl.BlockSpec((total, wide), lambda h, *_: (0, h))
    row = pl.BlockSpec((wide, total), lambda h, *_: (h, 0))
    sum_shapes, sum_specs, half_shapes, half_specs = [], [], [], []
    for keep, _ in sums:
        count, _, columns = keep.shape
        sum_specs += [pl.BlockSpec((count, wide, columns), lambda h, *_: (0, h, 0))] * 2
        half_specs += [pl.BlockSpec((count // 2, wide, columns), lambda h, *_: (0, h, 0))] * 2
        half_shapes += [jax.ShapeDtypeStruct((count // 2, width, columns), BF16)] * 2
    outs = pl.pallas_call(
        functools.partial(backward_kernel, group, len(sums)),
        out_shape=[jax.ShapeDtypeStruct((3, rows, width), BF16)] * group + half_shapes,
        grid_spec=pltpu.PrefetchScalarGridSpec(
            num_scalar_prefetch=1,
            grid=(heads // per,),
            in_specs=[
                column,
                column,
                pl.BlockSpec((per, total, total), lambda h, *_: (h, 0, 0)),
                row,
                column,
                column,
            ]
            + sum_specs,
            out_specs=[pl.BlockSpec((3, rows, wide), lambda h, *_: (0, 0, h))] * group
            + half_specs,
            scratch_shapes=[pltpu.VMEM((3, total, wide), BF16)],
        ),
        cost_estimate=light(),
        compiler_params=params(),
    )(table, grad, att, weights, q_t, k, v, *[x for pair in sums for x in pair])
    back, halves = outs[:group], outs[group:]
    return list(back), [halves[2 * c : 2 * c + 2] for c in range(len(sums))]


def block_rows(refs, columns):
    if len(refs) == 1:
        return refs[0][:, columns]
    own, near, inner, outer = refs
    return jnp.concatenate(
        [own[:, columns], near[:, columns], inner[:, columns] + outer[:, columns]], axis=0
    )


def block_columns(blocks, p, width):
    return pl.ds(pl.multiple_of(blocks[p] * width, LANES), width)


def project_kernel(count, pieces, first, *refs):
    weights, refs = refs[:pieces], refs[pieces:]
    rows, out = refs[:count], refs[-1]
    dp, _, unit = weights[0].shape
    part = unit * pieces
    total = None if first else refs[count][...]
    for p in range(dp):
        weight = jnp.concatenate([w[p] for w in weights], axis=1)
        term = dot(block_rows(rows, slice(p * part, (p + 1) * part)), weight, NT)
        total = term if total is None else total + term
    out[...] = total.astype(out.dtype)


def project(rows, weights, start, before, dtype, after=()):
    dp, heads, _ = weights.shape
    part = rows[0].shape[1] // dp
    unit = math.gcd(start, part)
    tokens = sum(r.shape[0] for r in rows[:3])
    before = [] if before is None else [before]
    at = range(start // unit, (start + part) // unit)
    return pl.pallas_call(
        functools.partial(project_kernel, len(rows), len(at), not before),
        out_shape=jax.ShapeDtypeStruct((tokens, heads), dtype),
        grid=(1,),
        in_specs=[pl.BlockSpec((dp, heads, unit), lambda i, c=c: (0, 0, c)) for c in at]
        + [whole(r.shape) for r in rows]
        + [whole(x.shape) for x in before]
        + awaited(after),
        out_specs=whole((tokens, heads)),
        cost_estimate=light(),
        compiler_params=params(),
    )(*[weights] * len(at), *rows, *before, *after)


def outer_kernel(count, start, passed, blocks, att_t_ref, *refs):
    rows = refs[:count]
    keep_ref, send_ref = refs[len(refs) - 2 - passed : len(refs) - passed]
    half, _, width = keep_ref.shape
    part = rows[0].shape[1] // (2 * half)
    att_t = att_t_ref[...]
    for p in range(2 * half):
        out = keep_ref if p < half else send_ref
        columns = pl.ds(pl.multiple_of(blocks[p] * part + start, LANES), width)
        out[p % half] = dot(att_t, block_rows(rows, columns)).astype(BF16)


def outer(blocks, att_t, rows, start, width, place, total, buffers=(), passed=()):
    half = blocks.shape[0] // 2
    heads = att_t.shape[0]
    first = 2 + len(rows)
    handed = list(buffers) + list(passed)
    outs = [jax.ShapeDtypeStruct((half, heads, total), BF16)] * 2
    aliases = {first + i: i for i in range(len(buffers))}
    aliases |= {first + len(buffers) + i: 2 + i for i in range(len(passed))}
    return pl.pallas_call(
        functools.partial(outer_kernel, len(rows), start, len(passed)),
        out_shape=outs + [jax.ShapeDtypeStruct(x.shape, x.dtype) for x in passed],
        grid_spec=pltpu.PrefetchScalarGridSpec(
            num_scalar_prefetch=1,
            grid=(1,),
            in_specs=[whole(att_t.shape)] + [whole(r.shape) for r in rows] + awaited(handed),
            out_specs=[pl.BlockSpec((half, heads, width), lambda i, b: (0, 0, place // width))] * 2
            + awaited(passed),
        ),
        input_output_aliases=aliases,
        cost_estimate=light(),
        compiler_params=params(),
    )(blocks, att_t, *rows, *handed)


def swap(value, axis, size, mask):
    return lax.ppermute(value, axis, [(i, i ^ mask) for i in range(size)])


def half_order(masks):
    order = [0]
    for mask in reversed(masks):
        order = order + [mask ^ r for r in order]
    return order


def fold(state, dp):
    kept, send, masks = state
    if not masks:
        return state
    kept = kept.astype(F32) + swap(send, "dp", dp, masks[0]).astype(F32)
    half = kept.shape[0] // 2
    if half == 0:
        return kept[0], kept[0], masks[1:]
    return kept[:half], kept[half:].astype(BF16), masks[1:]


def gather_rows(own, near, group, both=None, held=()):
    if group != 4:
        return [lax.all_gather(own, "head", axis=0, tiled=True)]
    inner = lax.ppermute(join(own, near) if both is None else both, "head", [(1, 2), (2, 1)])
    if held:
        inner = hold(inner, held)
    outer = lax.ppermute(inner, "head", [(1, 0), (2, 3)])
    return [own, near, inner, outer]


def local(
    dp,
    group,
    query_rows,
    key_rows,
    value_rows,
    out_grad,
    out_weight,
    token_order,
    tile_index,
    tile_count,
):
    table = tables(group, lax.axis_index("head"))
    up = [1 << i for i in range(dp.bit_length() - 1)]
    masks = [up, up[:1] + up[:0:-1]]
    widths = chunk_widths(out_weight.shape[1])

    def blocks(order):
        return jnp.bitwise_xor(lax.axis_index("dp"), jnp.array(half_order(order), jnp.int32))

    arrays = (query_rows, key_rows, value_rows)
    packed = pack(table, range(1, group), *arrays)
    parts = [swap(rows, "head", group, 1 + i) for i, rows in enumerate(packed)]
    parts = list(pack(table, [0], *arrays, after=parts[:1])) + parts
    pieces = split(out_grad, dp)
    nears = [swap(own, "head", group, 1) for own in pieces] if group == 4 else pieces
    both = join(pieces[0], nears[0], after=parts[1:])
    weights_full = lax.all_gather(out_weight, "dp", axis=0)

    tiles, counts = tile_index[0], tile_count[0]
    heads, cubes, slots = tiles.shape
    used = jnp.arange(slots, dtype=jnp.int32) < counts[:, :, None]
    listed = tiles[..., None] == jnp.arange(LANES, dtype=jnp.int32)
    allowed = jnp.any(listed & used[..., None], axis=2)
    bias = jnp.where(allowed, 0.0, masked_score).astype(BF16)
    bias = jnp.pad(bias, ((0, 0), (0, LANES - cubes), (0, 0)))

    att, att_t, weights, q_t, k, v = forward(table, token_order, bias, parts, after=[both])
    part = widths[0]
    cut = part // 2 if part % (2 * LANES) == 0 else 0
    order, other_order = blocks(masks[0]), blocks(masks[1])
    first = gather_rows(pieces[0], nears[0], group, both)
    grad = project(first, weights_full, 0, None, F32)
    state = outer(order, att_t, first, 0, part, 0, part + cut)
    second = gather_rows(pieces[1], nears[1], group, join(pieces[1], nears[1], after=[att_t]))
    third = gather_rows(pieces[2], nears[2], group, held=[grad, state[0]])
    grad = project(second, weights_full, part, grad, F32)
    if cut:
        state = outer(order, att_t, second, 0, cut, part, part + cut, state)
    rest = part - cut
    other = outer(other_order, att_t, second, cut, rest, part, part + rest)
    keep, send = state[0], hold(state[1], [third[-1]])
    *other, grad = outer(
        other_order, att_t, third, 0, part, 0, part + rest, other, passed=[grad]
    )
    grad = project(third, weights_full, 2 * part, grad, BF16, after=[other[0]])
    arrived = swap(send, "dp", dp, masks[0][0])
    other_arrived = swap(other[1], "dp", dp, masks[1][0])
    back, halves = backward(
        table, grad, att, weights, q_t, k, v, [(keep, arrived), (other[0], other_arrived)]
    )
    states = [(*half, mask[1:]) for half, mask in zip(halves, masks)]
    while any(masks for _, _, masks in states):
        states = [fold(state, dp) for state in states]
    back = [back[0]] + [swap(back[s], "head", group, s) for s in range(1, group)]
    low, high = [kept for kept, _, _ in states]
    total = jnp.concatenate([low, high[:, part:], high[:, :part]], axis=1).astype(BF16)
    query_back, key_back, value_back = unpack(table, back)
    return (att[None], query_back, key_back, value_back, total)


def solution(mesh):
    placed = (
        P("dp", "head", None),
        P("dp", "head", None),
        P("dp", "head", None),
        P("dp", "head", None),
        P("head", "dp"),
        P("dp", None),
        P("dp", "head", None, None),
        P("dp", "head", None),
    )
    return jax.shard_map(
        functools.partial(local, mesh.shape["dp"], mesh.shape["head"]),
        mesh=mesh,
        in_specs=placed,
        out_specs=(
            P("dp", None, "head"),
            P("dp", "head", None),
            P("dp", "head", None),
            P("dp", "head", None),
            P("head", "dp"),
        ),
        check_vma=False,
    )
```

```python
import functools
import math

import jax
import jax.numpy as jnp
from jax import lax
from jax.experimental import pallas as pl
from jax.experimental.pallas import tpu as pltpu
from jax.sharding import PartitionSpec as P

HEAD_DIM = 128
CUBE_TOKENS = 128
LANES = 128

masked_score = -1e30
scale = 1.0 / math.sqrt(HEAD_DIM)
log2_e = math.log2(math.e)

BF16 = jnp.bfloat16
F32 = jnp.float32
NT = (((1,), (1,)), ((), ()))
NN = (((1,), (0,)), ((), ()))


def chunk_widths(columns):
    return [columns // 3] * 3


def light():
    return pl.CostEstimate(flops=1, bytes_accessed=1, transcendentals=0)


def whole(shape):
    return pl.BlockSpec(shape, lambda *_: (0,) * len(shape))


def awaited(after):
    return [pl.BlockSpec(memory_space=pl.ANY)] * len(after)


def dot(a, b, dims=NN):
    return lax.dot_general(a, b, dims, preferred_element_type=F32)


def params(limit_mib=20):
    return pltpu.CompilerParams(vmem_limit_bytes=limit_mib * 1024 * 1024)


def tables(group, here):
    partner = jnp.bitwise_xor(here, jnp.arange(group, dtype=jnp.int32))
    if group != 4:
        return jnp.concatenate([partner, partner, jnp.arange(group, dtype=jnp.int32)])
    middle = jnp.logical_or(here == 1, here == 2)
    slots = jnp.where(middle, jnp.array([0, 1, 3, 2], jnp.int32), jnp.arange(4, dtype=jnp.int32))
    return jnp.concatenate([partner, slots, jnp.bitwise_xor(here, slots)])


def slot(table, s):
    return table[table.shape[0] // 3 + s]


def owner(table, t):
    return table[table.shape[0] // 3 * 2 + t]


def pack_kernel(group, table, *refs):
    ins, outs = refs[: 3 * group], refs[-group:]
    for s, out in enumerate(outs):
        for i in range(3):
            out[i] = ins[3 * s + i][0]


def pack(place, partners, q, k, v, after=()):
    group = place.shape[0]
    rows, total = q.shape[1:]
    shape = (3, rows, total // group)
    in_specs = []
    for s in partners:
        in_specs += [
            pl.BlockSpec((1, rows, total // group), lambda i, t, s=s: (0, 0, t[s]))
        ] * 3
    return pl.pallas_call(
        functools.partial(pack_kernel, len(partners)),
        out_shape=[jax.ShapeDtypeStruct(shape, BF16)] * len(partners),
        grid_spec=pltpu.PrefetchScalarGridSpec(
            num_scalar_prefetch=1,
            grid=(1,),
            in_specs=in_specs + awaited(after),
            out_specs=[whole(shape)] * len(partners),
        ),
        cost_estimate=light(),
        compiler_params=params(60),
    )(place, *[q, k, v] * len(partners), *after)


def split_kernel(dp, g_ref, *outs):
    columns = g_ref.shape[2] // dp
    before = 0
    for out in outs:
        part = out.shape[1] // dp
        for d in range(dp):
            start = d * columns + before
            out[:, d * part : (d + 1) * part] = g_ref[0, :, start : start + part]
        before += part


def split(g, dp):
    shapes = [(g.shape[1], width * dp) for width in chunk_widths(g.shape[2] // dp)]
    return pl.pallas_call(
        functools.partial(split_kernel, dp),
        out_shape=[jax.ShapeDtypeStruct(shape, BF16) for shape in shapes],
        grid=(1,),
        in_specs=[whole(g.shape)],
        out_specs=[whole(shape) for shape in shapes],
        cost_estimate=light(),
        compiler_params=params(),
    )(g)


def join_kernel(a_ref, b_ref, *refs):
    out = refs[-1]
    out[: a_ref.shape[0]] = a_ref[...]
    out[a_ref.shape[0] :] = b_ref[...]


def join(a, b, after=()):
    shape = (a.shape[0] + b.shape[0],) + a.shape[1:]
    return pl.pallas_call(
        join_kernel,
        out_shape=jax.ShapeDtypeStruct(shape, a.dtype),
        grid=(1,),
        in_specs=[whole(a.shape), whole(b.shape)] + awaited(after),
        out_specs=whole(shape),
        cost_estimate=light(),
        compiler_params=params(),
    )(a, b, *after)


def hold_kernel(*refs):
    pass


def hold(value, after):
    return pl.pallas_call(
        hold_kernel,
        out_shape=jax.ShapeDtypeStruct(value.shape, value.dtype),
        in_specs=awaited([value, *after]),
        out_specs=pl.BlockSpec(memory_space=pl.ANY),
        input_output_aliases={0: 0},
        cost_estimate=light(),
        compiler_params=params(),
    )(value, *after)


def unpack_first_kernel(partners, place, *refs):
    parts, outs = refs[: len(partners)], refs[-3:]
    width = parts[0].shape[2]
    for s, part in zip(partners, parts):
        columns = pl.ds(pl.multiple_of(place[s] * width, LANES), width)
        for i, out in enumerate(outs):
            out[0, :, columns] = part[i]


def unpack_last_kernel(count, place, *refs):
    for s, part in enumerate(refs[:count]):

        @pl.when(pl.program_id(0) == s)
        def _(part=part):
            for i, out in enumerate(refs[-3:]):
                out[0] = part[i]


def unpack(place, parts):
    group = place.shape[0] // 3
    _, rows, width = parts[0].shape
    shape = jax.ShapeDtypeStruct((1, rows, width * group), BF16)
    early = group // 2
    outs = pl.pallas_call(
        functools.partial(unpack_first_kernel, range(early)),
        out_shape=[shape] * 3,
        grid_spec=pltpu.PrefetchScalarGridSpec(
            num_scalar_prefetch=1,
            grid=(1,),
            in_specs=[whole(part.shape) for part in parts[:early]],
            out_specs=[whole(shape.shape)] * 3,
        ),
        cost_estimate=light(),
        compiler_params=params(),
    )(place, *parts[:early])
    late = parts[early:]
    return pl.pallas_call(
        functools.partial(unpack_last_kernel, len(late)),
        out_shape=[shape] * 3,
        grid_spec=pltpu.PrefetchScalarGridSpec(
            num_scalar_prefetch=1,
            grid=(len(late),),
            in_specs=[whole(part.shape) for part in late] + awaited(outs),
            out_specs=[pl.BlockSpec((1, rows, width), lambda i, t: (0, 0, t[early + i]))] * 3,
        ),
        input_output_aliases={1 + len(late) + i: i for i in range(3)},
        cost_estimate=light(),
        compiler_params=params(),
    )(place, *late, *outs)


def forward_kernel(group, table, order_ref, bias_ref, *refs):
    parts = refs[:group]
    att_ref, att_t_ref, weight_ref, q_t_ref, k_ref, v_ref, cube_ref, q_ref = refs[-8:]
    rows = parts[0].shape[1]
    total = q_ref.shape[0]

    @pl.when(pl.program_id(0) == 0)
    def _():
        position = lax.broadcasted_iota(jnp.int32, (total, LANES), 0)
        cube = lax.broadcasted_iota(jnp.int32, (total, LANES), 1)
        block = jnp.where(lax.div(position, CUBE_TOKENS) == cube, 1.0, 0.0).astype(BF16)
        for t in range(group):
            token = lax.broadcasted_iota(jnp.int32, (rows, total), 0) + owner(table, t) * rows
            onehot = jnp.where(token == order_ref[...], 1.0, 0.0).astype(BF16)
            cube_ref[t * rows : (t + 1) * rows, :] = dot(onehot, block).astype(BF16)

    for s, part in enumerate(parts):
        here = pl.ds(pl.multiple_of(slot(table, s) * rows, rows), rows)
        q_ref[here, :] = part[0]
        k_ref[here, :] = part[1]
        v_ref[here, :] = part[2]
    cubes = cube_ref[...]
    q, k, v = q_ref[...], k_ref[...], v_ref[...]
    bias = dot(cubes, bias_ref[0]).astype(BF16)
    scores = dot(
        jnp.concatenate([q, bias], axis=1), jnp.concatenate([k, cubes], axis=1), NT
    ) * (scale * log2_e)
    raised = jnp.exp2(scores - jnp.max(scores, axis=1, keepdims=True))
    weights = (raised * (1.0 / jnp.sum(raised, axis=1, keepdims=True))).astype(BF16)
    weight_ref[0] = weights
    output = dot(weights, v)
    for t in range(group):
        here = pl.ds(pl.multiple_of(owner(table, t) * rows, rows), rows)
        att_ref[here, :] = output[t * rows : (t + 1) * rows].astype(BF16)
    att_t_ref[...] = output.T.astype(BF16)
    q_t_ref[...] = q.astype(F32).T.astype(BF16)


def forward(table, order, bias, parts, after=()):
    group = len(parts)
    _, rows, width = parts[0].shape
    total = rows * group
    heads = width // HEAD_DIM
    column = pl.BlockSpec((total, HEAD_DIM), lambda h, *_: (0, h))
    row = pl.BlockSpec((HEAD_DIM, total), lambda h, *_: (h, 0))
    return pl.pallas_call(
        functools.partial(forward_kernel, group),
        out_shape=[
            jax.ShapeDtypeStruct((total, width), BF16),
            jax.ShapeDtypeStruct((width, total), BF16),
            jax.ShapeDtypeStruct((heads, total, total), BF16),
            jax.ShapeDtypeStruct((width, total), BF16),
            jax.ShapeDtypeStruct((total, width), BF16),
            jax.ShapeDtypeStruct((total, width), BF16),
        ],
        grid_spec=pltpu.PrefetchScalarGridSpec(
            num_scalar_prefetch=1,
            grid=(heads,),
            in_specs=[
                pl.BlockSpec((1, total), lambda h, *_: (0, 0)),
                pl.BlockSpec((1, LANES, LANES), lambda h, *_: (h, 0, 0)),
            ]
            + [pl.BlockSpec((3, rows, HEAD_DIM), lambda h, *_: (0, 0, h))] * group
            + awaited(after),
            out_specs=[
                column,
                row,
                pl.BlockSpec((1, total, total), lambda h, *_: (h, 0, 0)),
                row,
                column,
                column,
            ],
            scratch_shapes=[
                pltpu.VMEM((total, LANES), BF16),
                pltpu.VMEM((total, HEAD_DIM), BF16),
            ],
        ),
        cost_estimate=light(),
        compiler_params=params(),
    )(table, order, bias, *parts, *after)


def backward_kernel(
    group, chains, table, g_ref, att_ref, weight_ref, q_t_ref, k_ref, v_ref, *refs
):
    sums, refs = refs[: 2 * chains], refs[2 * chains :]
    outs, folded, held = refs[:group], refs[group:-1], refs[-1]
    rows = outs[0].shape[1]
    for i in range(weight_ref.shape[0]):
        one = slice(i * HEAD_DIM, (i + 1) * HEAD_DIM)
        grad = g_ref[:, one]
        weights = weight_ref[i]
        grad_float = grad.astype(F32)
        att = jnp.concatenate(
            [
                att_ref[pl.ds(pl.multiple_of(owner(table, t) * rows, rows), rows), one]
                for t in range(group)
            ],
            axis=0,
        )
        delta = jnp.sum(grad_float * att.astype(F32), axis=1, keepdims=True)
        diff = (weights.astype(F32) * (dot(grad, v_ref[:, one], NT) - delta)).astype(BF16)
        held[0, :, one] = (dot(diff, k_ref[:, one]) * scale).astype(BF16)
        held[1, :, one] = (dot(q_t_ref[one, :], diff) * scale).T.astype(BF16)
        held[2, :, one] = dot(grad_float.T.astype(BF16), weights).T.astype(BF16)
    for s, out in enumerate(outs):
        here = pl.ds(pl.multiple_of(slot(table, s) * rows, rows), rows)
        out[...] = held[:, here, :]
    for c in range(chains):
        keep_ref, arrived_ref = sums[2 * c : 2 * c + 2]
        kept_ref, send_ref = folded[2 * c : 2 * c + 2]
        half = kept_ref.shape[0]
        kept_ref[...] = keep_ref[:half] + arrived_ref[:half]
        send_ref[...] = keep_ref[half:] + arrived_ref[half:]


def backward(table, grad, att, weights, q_t, k, v, sums):
    group = table.shape[0] // 3
    total, width = grad.shape
    rows = total // group
    heads = width // HEAD_DIM
    per = 2 if heads % 2 == 0 else 1
    wide = per * HEAD_DIM
    column = pl.BlockSpec((total, wide), lambda h, *_: (0, h))
    row = pl.BlockSpec((wide, total), lambda h, *_: (h, 0))
    sum_shapes, sum_specs, half_shapes, half_specs = [], [], [], []
    for keep, _ in sums:
        count, _, columns = keep.shape
        sum_specs += [pl.BlockSpec((count, wide, columns), lambda h, *_: (0, h, 0))] * 2
        half_specs += [pl.BlockSpec((count // 2, wide, columns), lambda h, *_: (0, h, 0))] * 2
        half_shapes += [jax.ShapeDtypeStruct((count // 2, width, columns), BF16)] * 2
    outs = pl.pallas_call(
        functools.partial(backward_kernel, group, len(sums)),
        out_shape=[jax.ShapeDtypeStruct((3, rows, width), BF16)] * group + half_shapes,
        grid_spec=pltpu.PrefetchScalarGridSpec(
            num_scalar_prefetch=1,
            grid=(heads // per,),
            in_specs=[
                column,
                column,
                pl.BlockSpec((per, total, total), lambda h, *_: (h, 0, 0)),
                row,
                column,
                column,
            ]
            + sum_specs,
            out_specs=[pl.BlockSpec((3, rows, wide), lambda h, *_: (0, 0, h))] * group
            + half_specs,
            scratch_shapes=[pltpu.VMEM((3, total, wide), BF16)],
        ),
        cost_estimate=light(),
        compiler_params=params(),
    )(table, grad, att, weights, q_t, k, v, *[x for pair in sums for x in pair])
    back, halves = outs[:group], outs[group:]
    return list(back), [halves[2 * c : 2 * c + 2] for c in range(len(sums))]


def block_rows(refs, columns):
    if len(refs) == 1:
        return refs[0][:, columns]
    own, near, inner, outer = refs
    return jnp.concatenate(
        [own[:, columns], near[:, columns], inner[:, columns] + outer[:, columns]], axis=0
    )


def block_columns(blocks, p, width):
    return pl.ds(pl.multiple_of(blocks[p] * width, LANES), width)


def project_kernel(count, pieces, first, *refs):
    weights, refs = refs[:pieces], refs[pieces:]
    rows, out = refs[:count], refs[-1]
    dp, _, unit = weights[0].shape
    part = unit * pieces
    total = None if first else refs[count][...]
    for p in range(dp):
        weight = jnp.concatenate([w[p] for w in weights], axis=1)
        term = dot(block_rows(rows, slice(p * part, (p + 1) * part)), weight, NT)
        total = term if total is None else total + term
    out[...] = total.astype(out.dtype)


def project(rows, weights, start, before, dtype, after=()):
    dp, heads, _ = weights.shape
    part = rows[0].shape[1] // dp
    unit = math.gcd(start, part)
    tokens = sum(r.shape[0] for r in rows[:3])
    before = [] if before is None else [before]
    at = range(start // unit, (start + part) // unit)
    return pl.pallas_call(
        functools.partial(project_kernel, len(rows), len(at), not before),
        out_shape=jax.ShapeDtypeStruct((tokens, heads), dtype),
        grid=(1,),
        in_specs=[pl.BlockSpec((dp, heads, unit), lambda i, c=c: (0, 0, c)) for c in at]
        + [whole(r.shape) for r in rows]
        + [whole(x.shape) for x in before]
        + awaited(after),
        out_specs=whole((tokens, heads)),
        cost_estimate=light(),
        compiler_params=params(),
    )(*[weights] * len(at), *rows, *before, *after)


def outer_kernel(count, start, passed, blocks, att_t_ref, *refs):
    rows = refs[:count]
    keep_ref, send_ref = refs[len(refs) - 2 - passed : len(refs) - passed]
    half, _, width = keep_ref.shape
    part = rows[0].shape[1] // (2 * half)
    att_t = att_t_ref[...]
    for p in range(2 * half):
        out = keep_ref if p < half else send_ref
        columns = pl.ds(pl.multiple_of(blocks[p] * part + start, LANES), width)
        out[p % half] = dot(att_t, block_rows(rows, columns)).astype(BF16)


def outer(blocks, att_t, rows, start, width, place, total, buffers=(), passed=()):
    half = blocks.shape[0] // 2
    heads = att_t.shape[0]
    first = 2 + len(rows)
    handed = list(buffers) + list(passed)
    outs = [jax.ShapeDtypeStruct((half, heads, total), BF16)] * 2
    aliases = {first + i: i for i in range(len(buffers))}
    aliases |= {first + len(buffers) + i: 2 + i for i in range(len(passed))}
    return pl.pallas_call(
        functools.partial(outer_kernel, len(rows), start, len(passed)),
        out_shape=outs + [jax.ShapeDtypeStruct(x.shape, x.dtype) for x in passed],
        grid_spec=pltpu.PrefetchScalarGridSpec(
            num_scalar_prefetch=1,
            grid=(1,),
            in_specs=[whole(att_t.shape)] + [whole(r.shape) for r in rows] + awaited(handed),
            out_specs=[pl.BlockSpec((half, heads, width), lambda i, b: (0, 0, place // width))] * 2
            + awaited(passed),
        ),
        input_output_aliases=aliases,
        cost_estimate=light(),
        compiler_params=params(),
    )(blocks, att_t, *rows, *handed)


def swap(value, axis, size, mask):
    return lax.ppermute(value, axis, [(i, i ^ mask) for i in range(size)])


def half_order(masks):
    order = [0]
    for mask in reversed(masks):
        order = order + [mask ^ r for r in order]
    return order


def fold(state, dp):
    kept, send, masks = state
    if not masks:
        return state
    kept = kept.astype(F32) + swap(send, "dp", dp, masks[0]).astype(F32)
    half = kept.shape[0] // 2
    if half == 0:
        return kept[0], kept[0], masks[1:]
    return kept[:half], kept[half:].astype(BF16), masks[1:]


def gather_rows(own, near, group, both=None, held=()):
    if group != 4:
        return [lax.all_gather(own, "head", axis=0, tiled=True)]
    inner = lax.ppermute(join(own, near) if both is None else both, "head", [(1, 2), (2, 1)])
    if held:
        inner = hold(inner, held)
    outer = lax.ppermute(inner, "head", [(1, 0), (2, 3)])
    return [own, near, inner, outer]


def local(
    dp,
    group,
    query_rows,
    key_rows,
    value_rows,
    out_grad,
    out_weight,
    token_order,
    tile_index,
    tile_count,
):
    table = tables(group, lax.axis_index("head"))
    up = [1 << i for i in range(dp.bit_length() - 1)]
    masks = [up, up[:1] + up[:0:-1]]
    widths = chunk_widths(out_weight.shape[1])

    def blocks(order):
        return jnp.bitwise_xor(lax.axis_index("dp"), jnp.array(half_order(order), jnp.int32))

    arrays = (query_rows, key_rows, value_rows)
    place = jnp.bitwise_xor(lax.axis_index("head"), jnp.arange(group, dtype=jnp.int32))
    packed = pack(place, range(1, group), *arrays)
    parts = [swap(rows, "head", group, 1 + i) for i, rows in enumerate(packed)]
    parts = list(pack(place, [0], *arrays, after=parts[:1])) + parts
    pieces = split(out_grad, dp)
    nears = [swap(own, "head", group, 1) for own in pieces[:2]] if group == 4 else pieces
    if group == 4:
        nears.append(swap(hold(pieces[2], [nears[1]]), "head", group, 1))
    both = join(pieces[0], nears[0], after=parts[1:])
    weights_full = lax.all_gather(out_weight, "dp", axis=0)

    tiles, counts = tile_index[0], tile_count[0]
    heads, cubes, slots = tiles.shape
    used = jnp.arange(slots, dtype=jnp.int32) < counts[:, :, None]
    listed = tiles[..., None] == jnp.arange(LANES, dtype=jnp.int32)
    allowed = jnp.any(listed & used[..., None], axis=2)
    bias = jnp.where(allowed, 0.0, masked_score).astype(BF16)
    bias = jnp.pad(bias, ((0, 0), (0, LANES - cubes), (0, 0)))

    att, att_t, weights, q_t, k, v = forward(table, token_order, bias, parts, after=[both])
    part = widths[0]
    cut = part // 2 if part % (2 * LANES) == 0 else 0
    order, other_order = blocks(masks[0]), blocks(masks[1])
    first = gather_rows(pieces[0], nears[0], group, both)
    grad = project(first, weights_full, 0, None, F32)
    state = outer(order, att_t, first, 0, part, 0, part + cut)
    second = gather_rows(pieces[1], nears[1], group, join(pieces[1], nears[1], after=[att_t]))
    third = gather_rows(pieces[2], nears[2], group, held=[grad, state[0]])
    grad = project(second, weights_full, part, grad, F32)
    if cut:
        state = outer(order, att_t, second, 0, cut, part, part + cut, state)
    rest = part - cut
    other = outer(other_order, att_t, second, cut, rest, part, part + rest)
    keep, send = state[0], hold(state[1], [third[-1]])
    *other, grad = outer(
        other_order, att_t, third, 0, part, 0, part + rest, other, passed=[grad]
    )
    grad = project(third, weights_full, 2 * part, grad, BF16, after=[other[0]])
    arrived = swap(send, "dp", dp, masks[0][0])
    other_arrived = swap(other[1], "dp", dp, masks[1][0])
    back, halves = backward(
        table, grad, att, weights, q_t, k, v, [(keep, arrived), (other[0], other_arrived)]
    )
    states = [(*half, mask[1:]) for half, mask in zip(halves, masks)]
    while any(masks for _, _, masks in states):
        states = [fold(state, dp) for state in states]
    back = [back[0]] + [swap(back[s], "head", group, s) for s in range(1, group)]
    low, high = [kept for kept, _, _ in states]
    total = jnp.concatenate([low, high[:, part:], high[:, :part]], axis=1).astype(BF16)
    query_back, key_back, value_back = unpack(table, back)
    return (att[None], query_back, key_back, value_back, total)


def solution(mesh):
    placed = (
        P("dp", "head", None),
        P("dp", "head", None),
        P("dp", "head", None),
        P("dp", "head", None),
        P("head", "dp"),
        P("dp", None),
        P("dp", "head", None, None),
        P("dp", "head", None),
    )
    return jax.shard_map(
        functools.partial(local, mesh.shape["dp"], mesh.shape["head"]),
        mesh=mesh,
        in_specs=placed,
        out_specs=(
            P("dp", None, "head"),
            P("dp", "head", None),
            P("dp", "head", None),
            P("dp", "head", None),
            P("head", "dp"),
        ),
        check_vma=False,
    )
```
